128 devices in a mesh: step: 8 (over y, core), seq: 16 (over z, x).
Axes of the slice: x: 4, y: 4, z: 4, core: 2. Of those that a mesh axis runs over, the one named last changes fastest.
Arguments:
- iterate: float32 [8, 4096, 2048], P('step', 'seq'), may hold values from -6 to 6
- query_key_value_weight: bfloat16 [2048, 16, 384], P(None, 'seq'), may hold values from -0.125 to 0.125
- modulation_down_weight: bfloat16 [2048, 256], replicated, may hold values from -0.125 to 0.125
- modulation_up_weight: bfloat16 [256, 6144], replicated, may hold values from -0.375 to 0.375
- action_embedding_matrix: bfloat16 [512, 2048], replicated, may hold values from -12 to 12
- action_token_index: int32 [12], replicated, may hold values from 0 to 511
- sched: int32 [36], replicated, may hold values from 55 to 1000, as said below
- window: int32 [9], replicated, may hold values from 0 to 35, as said below
Outputs:
- new_states: float32 [8, 4096, 2048], P('step', 'seq')
- velocity: float32 [8, 4096, 2048], P('step', 'seq')
The draws below stay inside these ranges and needn't reach their ends.
Inputs may be any that keep to these rules, and one draw needn't show every extreme that they name: `sched`: strictly decreasing; entry 0 is 1000 and neighbouring entries differ by 5 to 27. `window`: strictly increasing; the first entry is 0 and the last is 35.
All inputs are finite; a program needn't handle non-finite values.
Results may differ from the reference program's by a relative error of at most 0.011.
Values may be sent and summed in bfloat16 or wider, within the bound.
A program may use at most 128 MiB of HBM per device.

```python
import math
import jax
import jax.numpy as jnp
from jax import lax

MODEL_WIDTH = 2048
HEADS = 16
HD = 128
MODULATION_RANK = 256
ACT_VOCAB = 512
ACT_LEN = 12
SCHED = 36
WINDOW = 8
TOKENS = 4096


def draw_sched(key, part):
    key = jax.random.fold_in(key, 11)
    gaps = jax.random.randint(key, (SCHED - 1,), 5, 28).astype(jnp.int32)
    start = jnp.full((1,), 1000, jnp.int32)
    return jnp.concatenate([start, 1000 - jnp.cumsum(gaps).astype(jnp.int32)])


def draw_window(key, part):
    key = jax.random.fold_in(key, 23)
    inner = jax.random.permutation(key, SCHED - 2)[:WINDOW - 1].astype(jnp.int32) + 1
    inner = jnp.sort(inner)
    first = jnp.zeros((1,), jnp.int32)
    last = jnp.full((1,), SCHED - 1, jnp.int32)
    return jnp.concatenate([first, inner, last])


def with_ends(drawn, own_key, least, top_value):
    place = [jax.random.randint(jax.random.fold_in(own_key, axis), (), 0, length) for axis, length in enumerate(drawn.shape)]
    main_axis = drawn.shape.index(max(drawn.shape))
    next_to = place[:main_axis] + [(place[main_axis] + 1) % drawn.shape[main_axis]] + place[main_axis + 1:]
    return drawn.at[tuple(place)].set(least).at[tuple(next_to)].set(top_value)


def steps_of(own_key, dims, cuts, smallest, largest):
    level = 1.0
    for position, shards_of in cuts:
        steps = jax.random.uniform(jax.random.fold_in(jax.random.fold_in(own_key, 6), position), (shards_of,), jnp.float32, smallest / len(cuts), largest / len(cuts))
        level = level * jnp.repeat(jnp.exp(steps), dims[position] // shards_of).reshape((-1,) + (1,) * (len(dims) - 1 - position))
    return level


def scatter_about(stream_key, shape, scale, reach, pieces=(), kind=jnp.bfloat16):
    values = scale * jax.random.normal(stream_key, shape, jnp.float32)
    if pieces:
        values = values * steps_of(stream_key, shape, pieces, -0.22, 0.18)
    return jnp.clip(values, -reach, reach).astype(kind)


def setup_inputs(seed: int = 0) -> dict:
    arg_keys = jax.random.split(jax.random.key(seed), 9)
    return {
        "iterate": scatter_about(arg_keys[0], (WINDOW, TOKENS, MODEL_WIDTH), 1.0, 6.0, ((0, 8), (1, 16)), jnp.float32),
        "query_key_value_weight": scatter_about(arg_keys[1], (MODEL_WIDTH, HEADS, 3 * HD), MODEL_WIDTH ** -0.5, 0.125, ((1, 16),)),
        "modulation_down_weight": scatter_about(arg_keys[2], (MODEL_WIDTH, MODULATION_RANK), MODEL_WIDTH ** -0.5, 0.125),
        "modulation_up_weight": scatter_about(arg_keys[3], (MODULATION_RANK, 3 * MODEL_WIDTH), MODULATION_RANK ** -0.5, 0.375),
        "action_embedding_matrix": scatter_about(arg_keys[4], (ACT_VOCAB, MODEL_WIDTH), 2.0, 12.0),
        "action_token_index": with_ends(jax.random.randint(arg_keys[5], (ACT_LEN,), 0, ACT_VOCAB), jax.random.fold_in(arg_keys[5], 1), 0, ACT_VOCAB - 1).astype(jnp.int32),
        "sched": draw_sched(jax.random.fold_in(arg_keys[8], 71), 0),
        "window": draw_window(jax.random.fold_in(arg_keys[8], 71), 0),
    }


def embed_time(timestep_markers, hidden_width):
    half = hidden_width // 2
    freqs = jnp.exp(-math.log(10000.0) * jnp.arange(half, dtype=jnp.float32) / half)
    angles = timestep_markers[:, None] * freqs[None, :]
    return jnp.concatenate([jnp.cos(angles), jnp.sin(angles)], axis=1)

def apply_modulation(timestep_markers, action_embedding_matrix, action_token_index, modulation_down_weight, modulation_up_weight):
    hidden_width = action_embedding_matrix.shape[1]
    onehot = (action_token_index[:, None] == jnp.arange(action_embedding_matrix.shape[0], dtype=jnp.int32)[None, :]).astype(jnp.bfloat16)
    action_mean = lax.optimization_barrier(jnp.mean(jnp.dot(onehot, action_embedding_matrix, preferred_element_type=jnp.float32), axis=0))
    conditioning_vector = jax.nn.silu(embed_time(timestep_markers, hidden_width) + action_mean[None, :]).astype(jnp.bfloat16)
    reduced_rank_update = jnp.dot(conditioning_vector, modulation_down_weight, preferred_element_type=jnp.float32).astype(jnp.bfloat16)
    return jnp.dot(reduced_rank_update, modulation_up_weight, preferred_element_type=jnp.float32).reshape(timestep_markers.shape[0], 3, hidden_width)

def norm_shift(state, shift, scale):
    spread = jnp.sqrt(lax.optimization_barrier(jnp.mean(state * state, axis=-1, keepdims=True)) + 1e-06)
    return (state / spread * (1.0 + scale[None, :]) + shift[None, :]).astype(jnp.bfloat16)

def normalize_heads(projected):
    head_dim = projected.shape[-1] // 3
    queries = projected[..., :head_dim]
    keys = projected[..., head_dim:2 * head_dim]
    values = projected[..., 2 * head_dim:]
    queries = queries / jnp.sqrt(lax.optimization_barrier(jnp.mean(queries * queries, axis=-1, keepdims=True)) + 1e-06)
    keys = keys / jnp.sqrt(lax.optimization_barrier(jnp.mean(keys * keys, axis=-1, keepdims=True)) + 1e-06)
    return jnp.concatenate([queries, keys, values], axis=-1).astype(jnp.bfloat16)

def attend_heads(packed):
    count = packed.shape[0]
    head_dim = packed.shape[2] // 3
    block = math.gcd(count, 512)
    factor = 2.5 / math.sqrt(head_dim)

    def one_head(head):
        keys = head[:, head_dim:2 * head_dim]
        values = head[:, 2 * head_dim:]
        queries = head[:, :head_dim].reshape(count // block, block, head_dim)

        def one_block(query_rows):
            scores = jnp.einsum('qd,kd->qk', query_rows, keys, preferred_element_type=jnp.float32) * factor
            weights = jnp.exp(scores)
            total = lax.optimization_barrier(jnp.sum(weights, axis=1, keepdims=True))
            mixed = jnp.dot(weights.astype(jnp.bfloat16), values, preferred_element_type=jnp.float32) / total
            return mixed.astype(jnp.bfloat16)
        return lax.map(one_block, queries).reshape(count, head_dim)
    result = lax.map(one_head, jnp.moveaxis(packed, 1, 0))
    return jnp.transpose(result, (1, 0, 2))

def reference(iterate, query_key_value_weight, modulation_down_weight, modulation_up_weight, action_embedding_matrix, action_token_index, sched, window):
    timestep_markers = sched[window].astype(jnp.float32)
    sigma = timestep_markers / 1000.0
    delta = sigma[1:] - sigma[:-1]
    modulation_factors = apply_modulation(timestep_markers[:-1], action_embedding_matrix, action_token_index, modulation_down_weight, modulation_up_weight)
    flat_weight = query_key_value_weight.reshape(MODEL_WIDTH, HEADS * 3 * HD)

    def drift(pair):
        state, parts = pair
        normed = norm_shift(state, parts[0], parts[1])
        projected = jnp.dot(normed, flat_weight, preferred_element_type=jnp.float32).reshape(TOKENS, HEADS, 3 * HD)
        attended = attend_heads(normalize_heads(projected))
        return parts[2][None, :] * attended.reshape(TOKENS, MODEL_WIDTH).astype(jnp.float32)
    velocity = lax.map(drift, (iterate, modulation_factors))
    terms = delta[:, None, None] * velocity
    terms = terms.at[0].add(iterate[0])
    new_states = jnp.cumsum(terms, axis=0)
    return (new_states, velocity)
```

```python
import functools
import math

import jax
import jax.numpy as jnp
from jax import lax
from jax.experimental import pallas as pl
from jax.experimental.pallas import tpu as pltpu
from jax.sharding import PartitionSpec as P

MESH = pl.DeviceIdType.MESH
F32, BF16 = jnp.float32, jnp.bfloat16


def place():
    step, seq = lax.axis_index("step"), lax.axis_index("seq")
    return step // 2, step % 2, seq // 4, seq % 4


def at(dy=0, dc=0, dz=0, dx=0):
    y, c, z, x = place()
    return (
        lax.rem(y + dy + 4, 4) * 2 + lax.rem(c + dc, 2),
        lax.rem(z + dz + 4, 4) * 4 + lax.rem(x + dx + 4, 4),
    )


def remote(src, dst, send, recv, device):
    return pltpu.make_async_remote_copy(
        src_ref=src, dst_ref=dst, send_sem=send, recv_sem=recv, device_id=device, device_id_type=MESH
    )


PARTNERS = (
    dict(dx=1), dict(dx=-1), dict(dz=1), dict(dz=-1), dict(dz=2),
    dict(dy=1), dict(dy=-1), dict(dy=2), dict(dc=1),
)


def project_kernel(
    x_ref, shift_ref, scale_ref, w_ref, out_ref,
    wbuf, xbuf, xm, stage, wl, w1s, w1r, w2s, w2r, wcs, wcr, xs, xr, fs, fr, qs, qr,
):
    y, c, z, x = place()
    barrier = pltpu.get_barrier_semaphore()
    for partner in PARTNERS:
        pl.semaphore_signal(barrier, inc=1, device_id=at(**partner), device_id_type=MESH)
    pl.semaphore_wait(barrier, len(PARTNERS))

    eighth = pl.ds(pl.multiple_of((c * 4 + y) * 256, 256), 256)
    half = pl.ds(pl.multiple_of(c * 1024, 1024), 1024)
    waits = []

    first = {}
    for j in (1, 3, 2):
        first[j] = remote(w_ref.at[eighth], wbuf.at[j, eighth], w1s.at[j], w1r.at[j], at(dz=-j))
        first[j].start()
        waits.append(first[j])
    own = pltpu.make_async_copy(w_ref, wbuf.at[0], wl)
    own.start()

    value = x_ref[...]
    spread = lax.rsqrt(jnp.mean(value * value, axis=-1, keepdims=True) + 1e-6)
    xbuf[0] = (value * spread).astype(BF16)
    top, bottom = pl.ds(0, 128), pl.ds(128, 128)
    toward = {}
    for part, rows in ((0, top), (1, bottom)):
        toward[3, part] = remote(xbuf.at[0, rows], xbuf.at[3, rows], xs.at[3, part], xr.at[3, part], at(dx=1))
    for part, rows in ((1, bottom), (0, top)):
        toward[1, part] = remote(xbuf.at[0, rows], xbuf.at[1, rows], xs.at[1, part], xr.at[1, part], at(dx=-1))
    for key in ((3, 0), (1, 1), (3, 1), (1, 0)):
        toward[key].start()
        waits.append(toward[key])

    def modulate(slot):
        xm[...] = (xbuf[slot].astype(F32) * (1.0 + scale_ref[...]) + shift_ref[...]).astype(BF16)

    second, sibling = {}, {}

    def spread_w(j):
        first[j].wait_recv()
        for i, dy in enumerate((1, -1, 2)):
            second[j, i] = remote(wbuf.at[j, eighth], wbuf.at[j, eighth], w2s.at[j, i], w2r.at[j, i], at(dy=dy))
            second[j, i].start()
            waits.append(second[j, i])

    def share_w(j):
        for i in range(3):
            second[j, i].wait_recv()
        sibling[j] = remote(wbuf.at[j, half], wbuf.at[j, half], wcs.at[j], wcr.at[j], at(dc=1))
        sibling[j].start()
        waits.append(sibling[j])

    factor = 2.5 / math.sqrt(128) * math.log2(math.e)
    outgoing = []

    def unit(block, j):
        p = jnp.dot(xm[...], wbuf[j], preferred_element_type=F32)
        q, k, v = p[:, :128], p[:, 128:256], p[:, 256:]
        q = q * (lax.rsqrt(jnp.mean(q * q, axis=-1, keepdims=True) + 1e-6) * factor)
        k = k * lax.rsqrt(jnp.mean(k * k, axis=-1, keepdims=True) + 1e-6)
        rows = pl.ds(pl.multiple_of((z * 4 + lax.rem(x + block, 4)) * 256, 256), 256)
        if j == 0:
            target = out_ref.at[rows]
        else:
            target = stage.at[j - 1, block]
        target[:, :128] = q.astype(BF16)
        target[:, 128:256] = k.astype(BF16)
        target[:, 256:] = v.astype(BF16)
        if j:
            copy = remote(stage.at[j - 1, block], out_ref.at[rows], qs.at[j - 1, block], qr.at[j - 1, block], at(dz=j))
            copy.start()
            outgoing.append(copy)

    modulate(0)
    spread_w(1)
    spread_w(3)
    spread_w(2)
    own.wait()
    unit(0, 0)
    toward[3, 0].wait_recv()
    fwd3 = remote(xbuf.at[3, top], xbuf.at[2, top], fs.at[0], fr.at[0], at(dx=1))
    fwd3.start()
    toward[1, 1].wait_recv()
    fwd1 = remote(xbuf.at[1, bottom], xbuf.at[2, bottom], fs.at[1], fr.at[1], at(dx=-1))
    fwd1.start()
    share_w(1)
    share_w(3)
    sibling[1].wait_recv()
    unit(0, 1)
    sibling[3].wait_recv()
    unit(0, 3)
    share_w(2)
    sibling[2].wait_recv()
    unit(0, 2)
    toward[3, 1].wait_recv()
    modulate(3)
    for j in (1, 3, 2, 0):
        unit(3, j)
    toward[1, 0].wait_recv()
    modulate(1)
    for j in (1, 3, 2, 0):
        unit(1, j)
    fwd3.wait_recv()
    fwd1.wait_recv()
    modulate(2)
    for j in (1, 3, 2, 0):
        unit(2, j)
    fwd3.wait_send()
    fwd1.wait_send()
    for copy in waits:
        copy.wait_send()
    for copy in outgoing:
        copy.wait()


def project(x, shift, scale, w):
    vm = pl.BlockSpec(memory_space=pltpu.VMEM)
    dma = pltpu.SemaphoreType.DMA
    return pl.pallas_call(
        project_kernel,
        out_shape=jax.ShapeDtypeStruct((4096, 384), BF16),
        in_specs=[vm, vm, vm, pl.BlockSpec(memory_space=pl.ANY)],
        out_specs=vm,
        scratch_shapes=[
            pltpu.VMEM((4, 2048, 384), BF16),
            pltpu.VMEM((4, 256, 2048), BF16),
            pltpu.VMEM((256, 2048), BF16),
            pltpu.VMEM((3, 4, 256, 384), BF16),
            dma, dma((4,)), dma((4,)), dma((4, 3)), dma((4, 3)), dma((4,)), dma((4,)),
            dma((4, 2)), dma((4, 2)), dma((2,)), dma((2,)), dma((3, 4)), dma((3, 4)),
        ],
        compiler_params=pltpu.CompilerParams(
            collective_id=1, has_side_effects=True, vmem_limit_bytes=56 * 1024 * 1024
        ),
    )(x, shift, scale, w)


def attend_kernel(pieces, kb, qkv, gd_ref, x_ref, mixed, pin, v1, ostage, pout, os, orr, ls, cs, cr):
    step, seq = lax.axis_index("step"), lax.axis_index("seq")
    R = 256 // pieces
    barrier = pltpu.get_barrier_semaphore()

    def peer(o):
        return (step, lax.rem(seq + o, 16))

    after = (lax.rem(step + 1, 8), seq)
    before = (lax.rem(step + 7, 8), seq)
    for o in range(1, 16):
        pl.semaphore_signal(barrier, inc=1, device_id=peer(o), device_id_type=MESH)
    for d in (after, before):
        pl.semaphore_signal(barrier, inc=1, device_id=d, device_id_type=MESH)
    v1[:, :128] = qkv[:, 256:]
    v1[:, 128:] = jnp.ones((4096, 128), BF16)
    pl.semaphore_wait(barrier, 17)
    mine = pl.ds(pl.multiple_of(seq * 128, 128), 128)

    def rows_of(p):
        return pl.ds(pl.multiple_of(p * R, R), R)

    def out_copy(p, o):
        to = lax.rem(seq + o, 16)
        return remote(ostage.at[p, to], mixed.at[rows_of(p), mine], os.at[p, o - 1], orr.at[p, o - 1], peer(o))

    def local_copy(p):
        return pltpu.make_async_copy(ostage.at[p, seq], mixed.at[rows_of(p), mine], ls.at[p])

    def chain_copy(p):
        return remote(pout.at[rows_of(p)], pin.at[rows_of(p)], cs.at[p], cr.at[p], after)

    def attend(p):
        q = jnp.concatenate([qkv[pl.ds(pl.multiple_of(s * 256 + p * R, R), R), :128] for s in range(16)], axis=0)
        acc = jnp.zeros((16 * R, 256), F32)
        for j in range(4096 // kb):
            s = lax.dot_general(q, qkv[j * kb:(j + 1) * kb, 128:256], (((1,), (1,)), ((), ())), preferred_element_type=F32)
            acc += jnp.dot(jnp.exp2(s).astype(BF16), v1[j * kb:(j + 1) * kb], preferred_element_type=F32)
        o = (acc[:, :128] / acc[:, 128:]).astype(BF16)
        for s in range(16):
            ostage[p, s] = o[s * R:(s + 1) * R]
        local_copy(p).start()
        for o in range(1, 16):
            out_copy(p, o).start()

    def chain(p):
        rows = rows_of(p)
        for o in range(1, 16):
            out_copy(p, o).wait_recv()
        local_copy(p).wait()

        @pl.when(step == 0)
        def _():
            pout[rows] = (x_ref[rows] + gd_ref[...] * mixed[rows].astype(F32)).astype(BF16)

        @pl.when(step > 0)
        def _():
            chain_copy(p).wait_recv()
            pout[rows] = (pin[rows].astype(F32) + gd_ref[...] * mixed[rows].astype(F32)).astype(BF16)

        @pl.when(step < 7)
        def _():
            chain_copy(p).start()

    def body(p, carry):
        attend(p)

        @pl.when(p > 0)
        def _():
            chain(p - 1)
        return carry

    lax.fori_loop(0, pieces, body, 0)
    chain(pieces - 1)

    @pl.when(step == 0)
    def _():
        pin[...] = jnp.zeros_like(pin)

    def drain(p, carry):
        for o in range(1, 16):
            out_copy(p, o).wait_send()

        @pl.when(step < 7)
        def _():
            chain_copy(p).wait_send()
        return carry

    lax.fori_loop(0, pieces, drain, 0)


def attend(qkv, gd, x, pieces=8, kb=4096):
    vm = pl.BlockSpec(memory_space=pltpu.VMEM)
    dma = pltpu.SemaphoreType.DMA
    R = 256 // pieces
    return pl.pallas_call(
        functools.partial(attend_kernel, pieces, kb),
        out_shape=(jax.ShapeDtypeStruct((256, 2048), BF16), jax.ShapeDtypeStruct((256, 2048), BF16)),
        in_specs=[vm, vm, vm],
        out_specs=(vm, vm),
        scratch_shapes=[
            pltpu.VMEM((4096, 256), BF16),
            pltpu.VMEM((pieces, 16, R, 128), BF16),
            pltpu.VMEM((256, 2048), BF16),
            dma((pieces, 15)), dma((pieces, 15)), dma((pieces,)), dma((pieces,)), dma((pieces,)),
        ],
        compiler_params=pltpu.CompilerParams(
            collective_id=2, has_side_effects=True, vmem_limit_bytes=56 * 1024 * 1024
        ),
    )(qkv, gd, x)


def embed_time(timestep_markers, hidden_width):
    half = hidden_width // 2
    freqs = jnp.exp(-math.log(10000.0) * jnp.arange(half, dtype=jnp.float32) / half)
    angles = timestep_markers[:, None] * freqs[None, :]
    return jnp.concatenate([jnp.cos(angles), jnp.sin(angles)], axis=1)


def apply_modulation(
    timestep_markers,
    action_embedding_matrix,
    action_token_index,
    modulation_down_weight,
    modulation_up_weight,
):
    hidden_width = action_embedding_matrix.shape[1]
    onehot = (
        action_token_index[:, None]
        == jnp.arange(action_embedding_matrix.shape[0], dtype=jnp.int32)[None, :]
    ).astype(jnp.bfloat16)
    action_mean = jnp.mean(
        jnp.dot(onehot, action_embedding_matrix, preferred_element_type=jnp.float32), axis=0
    )
    conditioning_vector = jax.nn.silu(
        embed_time(timestep_markers, hidden_width) + action_mean[None, :]
    ).astype(jnp.bfloat16)
    reduced_rank_update = jnp.dot(
        conditioning_vector, modulation_down_weight, preferred_element_type=jnp.float32
    ).astype(jnp.bfloat16)
    return jnp.dot(
        reduced_rank_update, modulation_up_weight, preferred_element_type=jnp.float32
    ).reshape(timestep_markers.shape[0], 3, hidden_width)


def on_device(
    iterate,
    query_key_value_weight,
    modulation_down_weight,
    modulation_up_weight,
    action_embedding_matrix,
    action_token_index,
    sched,
    window,
):
    step_count = iterate.shape[0]
    first_step = lax.axis_index("step") * step_count
    position = first_step + jnp.arange(step_count + 1, dtype=jnp.int32)
    chosen = jnp.sum(
        jnp.where(
            position[:, None] == jnp.arange(window.shape[0], dtype=jnp.int32)[None, :],
            window[None, :],
            0,
        ),
        axis=1,
    )
    stamps_int = jnp.sum(
        jnp.where(
            chosen[:, None] == jnp.arange(sched.shape[0], dtype=jnp.int32)[None, :],
            sched[None, :],
            0,
        ),
        axis=1,
    )
    timestep_markers = stamps_int.astype(jnp.float32)
    sigma = timestep_markers / 1000.0
    delta = sigma[1:] - sigma[:-1]
    modulation_factors = apply_modulation(
        timestep_markers[:-1],
        action_embedding_matrix,
        action_token_index,
        modulation_down_weight,
        modulation_up_weight,
    )
    shift, scale, gate = (modulation_factors[:, i] for i in range(3))
    rows = iterate[0]
    packed = project(rows, shift, scale, query_key_value_weight[:, 0])
    mixed, earlier = attend(packed, delta[:, None] * gate, rows)
    velocity = gate * mixed.astype(F32)
    entering = jnp.where(first_step == 0, rows, earlier.astype(F32))
    new_states = entering + delta[:, None] * velocity
    return (new_states[None], velocity[None])


def solution(mesh):
    placed = (P("step", "seq", None), P(None, "seq", None), P(), P(), P(), P(), P(), P())
    return jax.shard_map(
        on_device,
        mesh=mesh,
        in_specs=placed,
        out_specs=(P("step", "seq", None), P("step", "seq", None)),
        check_vma=False,
    )
```

```python
import math

import jax
import jax.numpy as jnp
from jax import lax
from jax.experimental import pallas as pl
from jax.experimental.pallas import tpu as pltpu
from jax.sharding import PartitionSpec as P

MESH = pl.DeviceIdType.MESH
F32, BF16 = jnp.float32, jnp.bfloat16
PIECES = 8
PIECE = 256 // PIECES
KEYS = 2048
FACTOR = 2.5 / math.sqrt(128) * math.log2(math.e)


def remote(src, dst, send, recv, device):
    return pltpu.make_async_remote_copy(
        src_ref=src, dst_ref=dst, send_sem=send, recv_sem=recv, device_id=device, device_id_type=MESH
    )


def inverse_rms(value):
    return lax.rsqrt(jnp.mean(value * value, axis=-1, keepdims=True) + 1e-6)


def sweep_kernel(
    ids, sched, window, x_ref, w_ref, ae_ref, md_ref, mu_ref,
    mixed, pin, gate_ref, delta_ref,
    xbuf, wraw, wmod, bias, ae, md, mu, qkv, v1, ostage, pout, gd,
    load_sem, home_s, home_r, guest_s, guest_r, share_s, share_r, wx_s, wx_r,
    hop_s, hop_r, out_s, out_r, chain_s, chain_r,
):
    step, seq = lax.axis_index("step"), lax.axis_index("seq")
    y, c = step // 2, lax.rem(step, 2)
    z, x = seq // 4, lax.rem(seq, 4)
    m = x // 2
    stays = c == m
    head = jnp.where(c == 0, seq, z * 4 + 3 - x)

    def device(core, dz, column):
        return (y * 2 + core, lax.rem(z + dz + 4, 4) * 4 + column)

    mate = device(c, 0, x + 1 - 2 * lax.rem(x, 2))
    up, down = device(c, 1, x), device(c, -1, x)
    sibling = device(1 - c, 0, x)
    across = [device(core, 0, 3 - x) for core in range(2)]
    after = (lax.rem(step + 1, 8), seq)
    before = (lax.rem(step + 7, 8), seq)

    barrier = pltpu.get_barrier_semaphore()
    for other in (mate, up, down, sibling, *across, after, before):
        pl.semaphore_signal(barrier, inc=1, device_id=other, device_id_type=MESH)
    for other_z in range(4):
        for column in range(2):
            for core in range(2):
                source = (y * 2 + core, other_z * 4 + 2 * c + column)
                itself = jnp.logical_and(core == c, other_z * 4 + 2 * c + column == seq)

                @pl.when(jnp.logical_not(itself))
                def _():
                    pl.semaphore_signal(barrier, inc=1, device_id=source, device_id_type=MESH)

    loads = [
        pltpu.make_async_copy(ae_ref, ae, load_sem.at[0]),
        pltpu.make_async_copy(md_ref, md, load_sem.at[1]),
        pltpu.make_async_copy(mu_ref, mu, load_sem.at[2]),
    ]
    for load in loads:
        load.start()
    own_w = pltpu.make_async_copy(w_ref, wraw, load_sem.at[3])

    @pl.when(c == 0)
    def _():
        own_w.start()

    mine = pl.ds(pl.multiple_of(c * 128, 128), 128)
    theirs = pl.ds(pl.multiple_of((1 - c) * 128, 128), 128)

    value = x_ref[...]
    unit = (value * inverse_rms(value)).astype(BF16)

    home_out = [
        remote(xbuf.at[0, theirs], xbuf.at[0, theirs], home_s.at[0], home_r.at[0], sibling),
        remote(xbuf.at[0, mine], xbuf.at[0, mine], home_s.at[1], home_r.at[1], sibling),
    ]
    guest_out = [
        remote(pout.at[pl.ds(core * 128, 128)], xbuf.at[1, pl.ds(core * 128, 128)], guest_s.at[core], guest_r, across[core])
        for core in range(2)
    ]

    pl.semaphore_wait(barrier, 8 + 16 - stays.astype(jnp.int32))

    @pl.when(stays)
    def _():
        xbuf[0] = unit
        home_out[0].start()

    @pl.when(jnp.logical_not(stays))
    def _():
        pout[...] = unit
        for copy in guest_out:
            copy.start()
        home_out[0].wait_recv()

    hops = []

    def hop(index, slot, to, to_slot, first=0, count=128):
        rows = pl.ds(pl.multiple_of(c * 128 + first, 32), count)
        copy = remote(xbuf.at[slot, rows], xbuf.at[to_slot, rows], hop_s.at[index], hop_r.at[index], to)
        hops.append(copy)
        return copy

    shares = {}

    def share(slot):
        shares[slot] = remote(xbuf.at[slot, mine], xbuf.at[slot, mine], share_s.at[slot], share_r.at[slot], sibling)
        shares[slot].start()

    h01 = hop(0, 0, mate, 2)
    h30 = hop(1, 0, up, 12)
    h10 = hop(2, 0, down, 4)
    for copy in (h01, h30, h10):
        copy.start()

    @pl.when(stays)
    def _():
        home_out[1].start()

    stamps = [sched[window[2 * y + i]].astype(F32) for i in range(3)]
    row8 = lax.broadcasted_iota(jnp.int32, (8, 1024), 0)
    lane = lax.broadcasted_iota(jnp.int32, (8, 1024), 1).astype(F32)
    angles = jnp.where(row8 == 0, stamps[0], stamps[1]) * jnp.exp(-math.log(10000.0) / 1024 * lane)
    temb = jnp.concatenate([jnp.cos(angles), jnp.sin(angles)], axis=1)
    vocab = lax.broadcasted_iota(jnp.int32, (16, 512), 1)
    counts = jnp.zeros((16, 512), F32)
    for i in range(12):
        counts += (vocab == ids[i]).astype(F32)
    for load in loads:
        load.wait()
    mean = jnp.dot(counts.astype(BF16), ae[...], preferred_element_type=F32)[:8] / 12.0
    cond = temb + mean
    cond = (cond / (1.0 + jnp.exp(-cond))).astype(BF16)
    low = jnp.dot(cond, md[...], preferred_element_type=F32).astype(BF16)
    factors = jnp.dot(low, mu[...], preferred_element_type=F32)
    scale_cols = lax.dot_general(
        mu[:, 2048:4096], low, (((0,), (1,)), ((), ())), preferred_element_type=F32
    )
    rows = lax.broadcasted_iota(jnp.int32, (8, 2048), 0)
    gate = jnp.sum(jnp.where(rows == c, factors[:, 4096:], 0.0), axis=0, keepdims=True)
    delta = jnp.where(c == 0, stamps[1] / 1000.0 - stamps[0] / 1000.0, stamps[2] / 1000.0 - stamps[1] / 1000.0)
    gate_ref[...] = gate
    delta_ref[...] = jnp.full((1, 128), delta, F32)
    gd[...] = gate * delta
    columns = lax.broadcasted_iota(jnp.int32, (2048, 8), 1)
    scale = jnp.sum(jnp.where(columns == m, scale_cols, 0.0), axis=1, keepdims=True)
    shift = factors[:, :2048]
    shift_high = shift.astype(BF16)
    shift_low = (shift - shift_high.astype(F32)).astype(BF16)

    guest_out[0].wait_recv()
    g01, g30, g10 = hop(3, 1, mate, 3), hop(4, 1, up, 13), hop(5, 1, down, 5)
    for copy in (g01, g30, g10):
        copy.start()
    w_across = remote(w_ref, wraw, wx_s, wx_r, across[1])

    @pl.when(c == 1)
    def _():
        w_across.start()

    share(1)
    h30.wait_recv()
    h20, x31h = hop(6, 12, up, 8), hop(7, 12, mate, 14)
    h20.start()
    x31h.start()
    share(12)
    h10.wait_recv()
    x11h = hop(8, 4, mate, 6)
    x11h.start()
    share(4)
    h01.wait_recv()
    share(2)

    g01.wait_recv()
    g31, g11 = hop(9, 3, up, 15), hop(10, 3, down, 7)
    g31.start()
    g11.start()
    share(3)
    g10.wait_recv()
    g20 = hop(11, 5, down, 9)
    g20.start()
    share(5)
    g30.wait_recv()
    share(13)

    @pl.when(c == 0)
    def _():
        own_w.wait()

    @pl.when(c == 1)
    def _():
        w_across.wait_recv()

    for i in range(4):
        part = pl.ds(i * 512, 512)
        wmod[part] = (wraw[part].astype(F32) * (1.0 + scale[i * 512:(i + 1) * 512])).astype(BF16)
    shifted = jnp.dot(shift_high, wraw[...], preferred_element_type=F32)
    shifted += jnp.dot(shift_low, wraw[...], preferred_element_type=F32)
    rows = lax.broadcasted_iota(jnp.int32, (8, 384), 0)
    bias[...] = jnp.sum(jnp.where(rows == m, shifted, 0.0), axis=0, keepdims=True)
    v1[:, 128:] = jnp.ones((4096, 128), BF16)

    def project(slot):
        zr, kind = slot // 4, slot % 4
        other = x + 1 - 2 * lax.rem(x, 2)
        column = (x, 3 - x, other, 3 - other)[kind]
        block = lax.rem(z + zr, 4) * 4 + column
        p = jnp.dot(xbuf[slot], wmod[...], preferred_element_type=F32) + bias[...]
        q, k = p[:, :128], p[:, 128:256]
        rows = pl.ds(pl.multiple_of(block * 256, 256), 256)
        qkv[rows, :128] = (q * (inverse_rms(q) * FACTOR)).astype(BF16)
        qkv[rows, 128:] = (k * inverse_rms(k)).astype(BF16)
        v1[rows, :128] = p[:, 256:].astype(BF16)

    @pl.when(jnp.logical_not(stays))
    def _():
        home_out[1].wait_recv()

    project(0)
    for slot in (1, 12, 4, 2):
        shares[slot].wait_recv()
        project(slot)

    x11h.wait_recv()
    part11 = hop(12, 6, down, 10, 32, 32)
    part11.start()
    share(6)
    h20.wait_recv()
    part20 = hop(13, 8, mate, 10, 64, 64)
    part20.start()
    share(8)
    g20.wait_recv()
    share(9)
    for slot in (3, 5, 13):
        shares[slot].wait_recv()
        project(slot)
    x31h.wait_recv()
    part31 = hop(14, 14, up, 10, 0, 32)
    part31.start()
    share(14)
    g31.wait_recv()
    part31g = hop(15, 15, up, 11, 0, 64)
    part31g.start()
    share(15)
    g11.wait_recv()
    part11g = hop(16, 7, down, 11, 64, 64)
    part11g.start()
    share(7)
    for slot in (6, 8, 9):
        shares[slot].wait_recv()
        project(slot)
    for slot in (14, 15, 7):
        shares[slot].wait_recv()
        project(slot)
    part31.wait_recv()
    part11.wait_recv()
    part20.wait_recv()
    share(10)
    part31g.wait_recv()
    part11g.wait_recv()
    share(11)
    for slot in (10, 11):
        shares[slot].wait_recv()
        project(slot)
    for copy in hops:
        copy.wait_send()
    for slot in shares:
        shares[slot].wait_send()

    @pl.when(stays)
    def _():
        for copy in home_out:
            copy.wait_send()

    @pl.when(jnp.logical_not(stays))
    def _():
        for copy in guest_out:
            copy.wait_send()

    @pl.when(c == 1)
    def _():
        w_across.wait_send()

    own_columns = pl.ds(pl.multiple_of(head * 128, 128), 128)

    def rows_of(p):
        return pl.ds(pl.multiple_of(p * PIECE, PIECE), PIECE)

    def out_copy(p, o):
        to = lax.rem(seq + o, 16)
        return remote(
            ostage.at[p, to], mixed.at[rows_of(p), own_columns], out_s.at[p, o], out_r.at[p, head], (y * 2 + m, to)
        )

    def keep_copy(p):
        return pltpu.make_async_copy(ostage.at[p, seq], mixed.at[rows_of(p), own_columns], out_r.at[p, head])

    def arrival(p, other):
        columns = pl.ds(other * 128, 128)
        return pltpu.make_async_copy(ostage.at[p, 0], mixed.at[rows_of(p), columns], out_r.at[p, other])

    def chain_copy(p):
        return remote(pout.at[rows_of(p)], pin.at[rows_of(p)], chain_s.at[p], chain_r.at[p], after)

    def attend(p):
        q = jnp.concatenate(
            [qkv[pl.ds(pl.multiple_of(s * 256 + p * PIECE, PIECE), PIECE), :128] for s in range(16)], axis=0
        )
        acc = jnp.zeros((16 * PIECE, 256), F32)
        for j in range(0, 4096, KEYS):
            s = lax.dot_general(
                q, qkv[j:j + KEYS, 128:], (((1,), (1,)), ((), ())), preferred_element_type=F32
            )
            acc += jnp.dot(jnp.exp2(s).astype(BF16), v1[j:j + KEYS], preferred_element_type=F32)
        o = (acc[:, :128] / acc[:, 128:]).astype(BF16)
        for s in range(16):
            ostage[p, s] = o[s * PIECE:(s + 1) * PIECE]

        @pl.when(stays)
        def _():
            keep_copy(p).start()

        @pl.when(jnp.logical_not(stays))
        def _():
            out_copy(p, 0).start()

        for o in range(1, 16):
            out_copy(p, o).start()

    def chain(p):
        rows = rows_of(p)
        for other in range(16):
            arrival(p, other).wait()

        @pl.when(step == 0)
        def _():
            pout[rows] = (x_ref[rows] + gd[...] * mixed[rows].astype(F32)).astype(BF16)

        @pl.when(step > 0)
        def _():
            chain_copy(p).wait_recv()
            pout[rows] = (pin[rows].astype(F32) + gd[...] * mixed[rows].astype(F32)).astype(BF16)

        @pl.when(step < 7)
        def _():
            chain_copy(p).start()

    def body(p, carry):
        attend(p)

        @pl.when(p > 0)
        def _():
            chain(p - 1)
        return carry

    lax.fori_loop(0, PIECES, body, 0)
    chain(PIECES - 1)

    @pl.when(step == 0)
    def _():
        pin[...] = jnp.zeros_like(pin)

    def drain(p, carry):
        @pl.when(jnp.logical_not(stays))
        def _():
            out_copy(p, 0).wait_send()

        for o in range(1, 16):
            out_copy(p, o).wait_send()

        @pl.when(step < 7)
        def _():
            chain_copy(p).wait_send()
        return carry

    lax.fori_loop(0, PIECES, drain, 0)


def sweep(ids, sched, window, x, w, ae, md, mu):
    vm = pl.BlockSpec(memory_space=pltpu.VMEM)
    sm = pl.BlockSpec(memory_space=pltpu.SMEM)
    anywhere = pl.BlockSpec(memory_space=pl.ANY)
    dma = pltpu.SemaphoreType.DMA
    return pl.pallas_call(
        sweep_kernel,
        out_shape=(
            jax.ShapeDtypeStruct((256, 2048), BF16), jax.ShapeDtypeStruct((256, 2048), BF16),
            jax.ShapeDtypeStruct((1, 2048), F32), jax.ShapeDtypeStruct((1, 128), F32),
        ),
        in_specs=[sm, sm, sm, vm, anywhere, anywhere, anywhere, anywhere],
        out_specs=(vm, vm, vm, vm),
        scratch_shapes=[
            pltpu.VMEM((16, 256, 2048), BF16),
            pltpu.VMEM((2048, 384), BF16),
            pltpu.VMEM((2048, 384), BF16),
            pltpu.VMEM((1, 384), F32),
            pltpu.VMEM((512, 2048), BF16),
            pltpu.VMEM((2048, 256), BF16),
            pltpu.VMEM((256, 6144), BF16),
            pltpu.VMEM((4096, 256), BF16),
            pltpu.VMEM((4096, 256), BF16),
            pltpu.VMEM((PIECES, 16, PIECE, 128), BF16),
            pltpu.VMEM((256, 2048), BF16),
            pltpu.VMEM((1, 2048), F32),
            dma((4,)), dma((2,)), dma((2,)), dma((2,)), dma, dma((16,)), dma((16,)), dma, dma,
            dma((17,)), dma((17,)), dma((PIECES, 16)), dma((PIECES, 16)), dma((PIECES,)), dma((PIECES,)),
        ],
        compiler_params=pltpu.CompilerParams(
            collective_id=1, has_side_effects=True, vmem_limit_bytes=60 * 1024 * 1024
        ),
    )(ids, sched, window, x, w, ae, md, mu)


def on_device(
    iterate,
    query_key_value_weight,
    modulation_down_weight,
    modulation_up_weight,
    action_embedding_matrix,
    action_token_index,
    sched,
    window,
):
    rows = iterate[0]
    mixed, earlier, gate, delta = sweep(
        action_token_index,
        sched,
        window,
        rows,
        query_key_value_weight[:, 0],
        action_embedding_matrix,
        modulation_down_weight,
        modulation_up_weight,
    )
    velocity = gate * mixed.astype(F32)
    entering = jnp.where(lax.axis_index("step") == 0, rows, earlier.astype(F32))
    new_states = entering + delta[:, :1] * velocity
    return (new_states[None], velocity[None])


def solution(mesh):
    placed = (P("step", "seq", None), P(None, "seq", None), P(), P(), P(), P(), P(), P())
    return jax.shard_map(
        on_device,
        mesh=mesh,
        in_specs=placed,
        out_specs=(P("step", "seq", None), P("step", "seq", None)),
        check_vma=False,
    )
```

```python
import math

import jax
import jax.numpy as jnp
from jax import lax
from jax.experimental import pallas as pl
from jax.experimental.pallas import tpu as pltpu
from jax.sharding import PartitionSpec as P

MESH = pl.DeviceIdType.MESH
F32, BF16 = jnp.float32, jnp.bfloat16
PIECES = 8
LAGS = ((3, "begin"), (5, "middle"), (7, "end"))
PIECE = 256 // PIECES
GROUPS = ((0, 1, 12, 4, 2), (3, 5, 13), (6, 8, 9), (14, 15, 7), (10, 11))
ORDER = sum(GROUPS, ())
FACTOR = 2.5 / math.sqrt(128) * math.log2(math.e)


def remote(src, dst, send, recv, device):
    return pltpu.make_async_remote_copy(
        src_ref=src, dst_ref=dst, send_sem=send, recv_sem=recv, device_id=device, device_id_type=MESH
    )


def inverse_rms(value):
    return lax.rsqrt(jnp.mean(value * value, axis=-1, keepdims=True) + 1e-6)


def sweep_kernel(
    ids, sched, window, x_ref, w_ref, ae_ref, md_ref, mu_ref,
    mixed, pin, gate_ref, delta_ref,
    xbuf, wraw, wmod, bias, ae, md, mu, qk, v1, acc, ostage, pout, gd, sout, tin, in0, in1,
    load_sem, home_s, home_r, guest_s, guest_r, share_s, share_r, wx_s, wx_r,
    hop_s, hop_r, out_s, out_r, t_s, t_r, s0_s, s0_r, s1_s, s1_r, e_s, e_r,
):
    step, seq = lax.axis_index("step"), lax.axis_index("seq")
    y, c = step // 2, lax.rem(step, 2)
    z, x = seq // 4, lax.rem(seq, 4)
    m = x // 2
    stays = c == m
    head = jnp.where(c == 0, seq, z * 4 + 3 - x)

    def device(core, dz, column):
        return (y * 2 + core, lax.rem(z + dz + 4, 4) * 4 + column)

    mate = device(c, 0, x + 1 - 2 * lax.rem(x, 2))
    up, down = device(c, 1, x), device(c, -1, x)
    sibling = device(1 - c, 0, x)
    across = [device(core, 0, 3 - x) for core in range(2)]
    planes = [(lax.rem(y + dy, 4) * 2 + c, seq) for dy in (1, 3, 2)]

    barrier = pltpu.get_barrier_semaphore()
    for other in (mate, up, down, sibling, *across, *planes):
        pl.semaphore_signal(barrier, inc=1, device_id=other, device_id_type=MESH)
    for other_z in range(4):
        for column in range(2):
            for core in range(2):
                source = (y * 2 + core, other_z * 4 + 2 * c + column)
                itself = jnp.logical_and(core == c, other_z * 4 + 2 * c + column == seq)

                @pl.when(jnp.logical_not(itself))
                def _():
                    pl.semaphore_signal(barrier, inc=1, device_id=source, device_id_type=MESH)

    loads = [
        pltpu.make_async_copy(ae_ref, ae, load_sem.at[0]),
        pltpu.make_async_copy(md_ref, md, load_sem.at[1]),
        pltpu.make_async_copy(mu_ref, mu, load_sem.at[2]),
    ]
    for load in loads:
        load.start()
    own_w = pltpu.make_async_copy(w_ref, wraw, load_sem.at[3])

    @pl.when(c == 0)
    def _():
        own_w.start()

    mine = pl.ds(pl.multiple_of(c * 128, 128), 128)
    theirs = pl.ds(pl.multiple_of((1 - c) * 128, 128), 128)

    home_out = [
        remote(xbuf.at[0, theirs], xbuf.at[0, theirs], home_s.at[0], home_r.at[0], sibling),
        remote(xbuf.at[0, mine], xbuf.at[0, mine], home_s.at[1], home_r.at[1], sibling),
    ]
    guest_out = [
        remote(pout.at[pl.ds(core * 128, 128)], xbuf.at[1, pl.ds(core * 128, 128)], guest_s.at[core], guest_r, across[core])
        for core in range(2)
    ]

    pl.semaphore_wait(barrier, 9 + 16 - stays.astype(jnp.int32))

    quarter = pl.ds(pl.multiple_of(y * 512, 512), 512)
    w_across = remote(w_ref.at[quarter], wraw.at[quarter], wx_s.at[0], wx_r.at[0], across[1])
    w_planes = [
        remote(wraw.at[quarter], wraw.at[quarter], wx_s.at[i + 1], wx_r.at[i + 1], planes[i]) for i in range(3)
    ]

    @pl.when(c == 1)
    def _():
        w_across.start()

    value = x_ref[...]
    unit = (value * inverse_rms(value)).astype(BF16)

    @pl.when(stays)
    def _():
        xbuf[0] = unit
        home_out[0].start()

    @pl.when(jnp.logical_not(stays))
    def _():
        pout[...] = unit
        for copy in guest_out:
            copy.start()
        home_out[0].wait_recv()

    hops = []

    def hop(index, slot, to, to_slot, first=0, count=128):
        rows = pl.ds(pl.multiple_of(c * 128 + first, 32), count)
        copy = remote(xbuf.at[slot, rows], xbuf.at[to_slot, rows], hop_s.at[index], hop_r.at[index], to)
        hops.append(copy)
        return copy

    shares = {}

    def share(slot):
        shares[slot] = remote(xbuf.at[slot, mine], xbuf.at[slot, mine], share_s.at[slot], share_r.at[slot], sibling)
        shares[slot].start()

    h01 = hop(0, 0, mate, 2)
    h30 = hop(1, 0, up, 12)
    h10 = hop(2, 0, down, 4)
    for copy in (h01, h30, h10):
        copy.start()

    @pl.when(stays)
    def _():
        home_out[1].start()

    stamps = [sched[window[2 * y + i]].astype(F32) for i in range(3)]
    row8 = lax.broadcasted_iota(jnp.int32, (8, 1024), 0)
    lane = lax.broadcasted_iota(jnp.int32, (8, 1024), 1).astype(F32)
    angles = jnp.where(row8 == 0, stamps[0], stamps[1]) * jnp.exp(-math.log(10000.0) / 1024 * lane)
    temb = jnp.concatenate([jnp.cos(angles), jnp.sin(angles)], axis=1)
    vocab = lax.broadcasted_iota(jnp.int32, (16, 512), 1)
    counts = jnp.zeros((16, 512), F32)
    for i in range(12):
        counts += (vocab == ids[i]).astype(F32)
    for load in loads:
        load.wait()
    mean = jnp.dot(counts.astype(BF16), ae[...], preferred_element_type=F32)[:8] / 12.0
    cond = temb + mean
    cond = (cond / (1.0 + jnp.exp(-cond))).astype(BF16)
    low = jnp.dot(cond, md[...], preferred_element_type=F32).astype(BF16)
    factors = jnp.dot(low, mu[...], preferred_element_type=F32)
    scale_cols = lax.dot_general(
        mu[:, 2048:4096], low, (((0,), (1,)), ((), ())), preferred_element_type=F32
    )
    rows = lax.broadcasted_iota(jnp.int32, (8, 2048), 0)
    gate = jnp.sum(jnp.where(rows == c, factors[:, 4096:], 0.0), axis=0, keepdims=True)
    delta = jnp.where(c == 0, stamps[1] / 1000.0 - stamps[0] / 1000.0, stamps[2] / 1000.0 - stamps[1] / 1000.0)
    gate_ref[...] = gate
    delta_ref[...] = jnp.full((1, 128), delta, F32)
    gd[...] = gate * delta
    columns = lax.broadcasted_iota(jnp.int32, (2048, 8), 1)
    scale = jnp.sum(jnp.where(columns == m, scale_cols, 0.0), axis=1, keepdims=True)
    shift = factors[:, :2048]
    shift_high = shift.astype(BF16)
    shift_low = (shift - shift_high.astype(F32)).astype(BF16)

    @pl.when(c == 1)
    def _():
        w_across.wait_recv()
        for copy in w_planes:
            copy.start()

    guest_out[0].wait_recv()
    g01, g30, g10 = hop(3, 1, mate, 3), hop(4, 1, up, 13), hop(5, 1, down, 5)
    for copy in (g01, g30, g10):
        copy.start()
    share(1)
    h30.wait_recv()
    h20, x31h = hop(6, 12, up, 8), hop(7, 12, mate, 14)
    h20.start()
    x31h.start()
    share(12)
    h10.wait_recv()
    x11h = hop(8, 4, mate, 6)
    x11h.start()
    share(4)
    h01.wait_recv()
    share(2)

    g01.wait_recv()
    g31, g11 = hop(9, 3, up, 15), hop(10, 3, down, 7)
    g31.start()
    g11.start()
    share(3)
    g10.wait_recv()
    g20 = hop(11, 5, down, 9)
    g20.start()
    share(5)
    g30.wait_recv()
    share(13)

    @pl.when(c == 0)
    def _():
        own_w.wait()

    @pl.when(c == 1)
    def _():
        for copy in w_planes:
            copy.wait_recv()

    for i in range(4):
        part = pl.ds(i * 512, 512)
        wmod[part] = (wraw[part].astype(F32) * (1.0 + scale[i * 512:(i + 1) * 512])).astype(BF16)
    shifted = jnp.dot(shift_high, wraw[...], preferred_element_type=F32)
    shifted += jnp.dot(shift_low, wraw[...], preferred_element_type=F32)
    rows = lax.broadcasted_iota(jnp.int32, (8, 384), 0)
    bias[...] = jnp.sum(jnp.where(rows == m, shifted, 0.0), axis=0, keepdims=True)
    v1[:, :, 128:] = jnp.ones((16, 256, 128), BF16)

    def block_of(slot):
        zr, kind = slot // 4, slot % 4
        other = x + 1 - 2 * lax.rem(x, 2)
        return lax.rem(z + zr, 4) * 4 + (x, 3 - x, other, 3 - other)[kind]

    def project(slot):
        place = ORDER.index(slot)
        p = jnp.dot(xbuf[slot], wmod[...], preferred_element_type=F32) + bias[...]
        q, k = p[:, :128], p[:, 128:256]
        qk[place, :, :128] = (q * (inverse_rms(q) * FACTOR)).astype(BF16)
        qk[place, :, 128:] = (k * inverse_rms(k)).astype(BF16)
        v1[place, :, :128] = p[:, 256:].astype(BF16)

    def weigh(q, first, last):
        keys = qk[first:last, :, 128:].reshape((last - first) * 256, 128)
        values = v1[first:last].reshape((last - first) * 256, 256)
        s = lax.dot_general(q, keys, (((1,), (1,)), ((), ())), preferred_element_type=F32)
        return jnp.dot(jnp.exp2(s).astype(BF16), values, preferred_element_type=F32)

    def fresh(first, last):
        count = last - first
        q = qk[first:last, :, :128].reshape(count * 256, 128)
        for at in range(0, last, 4):
            part = weigh(q, at, min(at + 4, last)).reshape(count, 256, 256)
            if at == 0:
                acc[first:last] = part
            else:
                acc[first:last] += part

    def extend(first, last):
        for half in range(2):
            rows = pl.ds(half * 128, 128)
            q = qk[:first, rows, :128].reshape(first * 128, 128)
            acc[:first, rows] += weigh(q, first, last).reshape(first, 128, 256)

    def absorb(group):
        first = ORDER.index(GROUPS[group][0])
        last = first + len(GROUPS[group])
        for slot in GROUPS[group]:
            if slot:
                shares[slot].wait_recv()
            else:
                @pl.when(jnp.logical_not(stays))
                def _():
                    home_out[1].wait_recv()
            project(slot)
        if group < len(GROUPS) - 1:
            if group:
                extend(first, last)
            fresh(first, last)

    absorb(0)
    absorb(1)
    x11h.wait_recv()
    part11 = hop(12, 6, down, 10, 32, 32)
    part11.start()
    share(6)
    h20.wait_recv()
    part20 = hop(13, 8, mate, 10, 64, 64)
    part20.start()
    share(8)
    g20.wait_recv()
    share(9)
    absorb(2)
    x31h.wait_recv()
    part31 = hop(14, 14, up, 10, 0, 32)
    part31.start()
    share(14)
    g31.wait_recv()
    part31g = hop(15, 15, up, 11, 0, 64)
    part31g.start()
    share(15)
    g11.wait_recv()
    part11g = hop(16, 7, down, 11, 64, 64)
    part11g.start()
    share(7)
    absorb(3)
    part31.wait_recv()
    part11.wait_recv()
    part20.wait_recv()
    share(10)
    part31g.wait_recv()
    part11g.wait_recv()
    share(11)
    absorb(4)
    fresh(14, 16)

    @pl.when(jnp.logical_not(stays))
    def _():
        for copy in guest_out:
            copy.wait_send()


    own_columns = pl.ds(pl.multiple_of(head * 128, 128), 128)
    dests = [block_of(slot) for slot in ORDER]

    def rows_of(p):
        return pl.ds(pl.multiple_of(p * PIECE, PIECE), PIECE)

    def out_copy(p, place):
        return remote(
            ostage.at[p, place], mixed.at[rows_of(p), own_columns], out_s, out_r.at[p], (y * 2 + m, dests[place])
        )

    def keep_copy(p):
        return pltpu.make_async_copy(ostage.at[p, 0], mixed.at[rows_of(p), own_columns], out_r.at[p])

    def finish(p):
        rows = rows_of(p)
        q = qk[:14, rows, :128].reshape(14 * PIECE, 128)
        early = acc[:14, rows].reshape(14 * PIECE, 256) + weigh(q, 14, 16)
        late = acc[14:, rows].reshape(2 * PIECE, 256)
        ostage[p, :14] = (early[:, :128] / early[:, 128:]).astype(BF16).reshape(14, PIECE, 128)
        ostage[p, 14:] = (late[:, :128] / late[:, 128:]).astype(BF16).reshape(2, PIECE, 128)

        @pl.when(stays)
        def _():
            keep_copy(p).start()

        @pl.when(jnp.logical_not(stays))
        def _():
            out_copy(p, 0).start()

        for place in range(1, 16):
            out_copy(p, place).start()

    def hand(src, dst, send, recv, p, to):
        return remote(src.at[rows_of(p)], dst.at[rows_of(p)], send.at[p], recv.at[p], to)

    above, below, _ = planes
    term_copy = lambda p: hand(pout, tin, t_s, t_r, p, sibling)
    sum_up = lambda p: hand(sout, in0, s0_s, s0_r, p, above)
    sum_wrap = lambda p: hand(sout, in0, s1_s, s0_r, p, below)
    sum_next = lambda p: hand(sout, in1, s1_s, s1_r, p, above)
    pass_down = lambda p: hand(in0, in0, s0_s, s0_r, p, below)
    back_in0 = lambda p: hand(in0, pin, e_s, e_r, p, sibling)
    back_pout = lambda p: hand(pout, pin, e_s, e_r, p, sibling)

    def load(ref, p):
        return ref[rows_of(p)].astype(F32)

    def begin(p):
        rows = rows_of(p)
        pltpu.make_async_copy(mixed.at[rows], mixed.at[rows], out_r.at[p]).wait()
        term = gd[...] * load(mixed, p)

        @pl.when(c == 0)
        def _():
            @pl.when(y == 0)
            def _():
                pout[rows] = (x_ref[rows] + term).astype(BF16)

            @pl.when(y > 0)
            def _():
                pout[rows] = term.astype(BF16)

            term_copy(p).start()

        @pl.when(c == 1)
        def _():
            term_copy(p).wait_recv()

            @pl.when(y < 2)
            def _():
                sout[rows] = (load(tin, p) + term).astype(BF16)

            @pl.when(y == 0)
            def _():
                sum_up(p).start()
                sum_wrap(p).start()

            @pl.when(y == 1)
            def _():
                sum_next(p).start()

            @pl.when(y == 2)
            def _():
                sout[rows] = (load(tin, p) + term).astype(BF16)

    def middle(p):
        rows = rows_of(p)

        @pl.when(jnp.logical_and(c == 1, y == 2))
        def _():
            sum_next(p).wait_recv()
            sout[rows] = (load(in1, p) + load(sout, p)).astype(BF16)
            sum_next(p).start()

        @pl.when(jnp.logical_and(c == 1, y == 3))
        def _():
            sum_up(p).wait_recv()
            pass_down(p).start()

    def end(p):
        rows = rows_of(p)

        @pl.when(jnp.logical_and(c == 0, y > 0))
        def _():
            back_in0(p).wait_recv()

        @pl.when(jnp.logical_and(c == 1, y == 0))
        def _():
            pin[rows] = tin[rows]

        @pl.when(jnp.logical_and(c == 1, y == 1))
        def _():
            sum_up(p).wait_recv()
            back_in0(p).start()
            pin[rows] = (load(in0, p) + load(tin, p)).astype(BF16)

        @pl.when(jnp.logical_and(c == 1, y > 1))
        def _():
            @pl.when(y == 2)
            def _():
                pass_down(p).wait_recv()

            @pl.when(y == 3)
            def _():
                sum_next(p).wait_recv()

            total = load(in0, p) + load(in1, p)
            pout[rows] = total.astype(BF16)
            back_pout(p).start()
            pin[rows] = (total + load(tin, p)).astype(BF16)

    def body(p, carry):
        @pl.when(p < PIECES)
        def _():
            finish(p)

        for lag, part in LAGS:
            @pl.when(jnp.logical_and(p >= lag, p < PIECES + lag))
            def _(lag=lag, part=part):
                stages[part](p - lag)
        return carry

    stages = {"begin": begin, "middle": middle, "end": end}
    lax.fori_loop(0, PIECES + LAGS[-1][0], body, 0)

    @pl.when(step == 0)
    def _():
        pin[...] = jnp.zeros_like(pin)

    for copy in hops:
        copy.wait_send()
    for slot in shares:
        shares[slot].wait_send()

    @pl.when(stays)
    def _():
        for copy in home_out:
            copy.wait_send()
        pltpu.make_async_copy(ostage.at[:, 1:], ostage.at[:, 1:], out_s).wait()

    @pl.when(jnp.logical_not(stays))
    def _():
        pltpu.make_async_copy(ostage, ostage, out_s).wait()

    @pl.when(c == 1)
    def _():
        w_across.wait_send()
        for copy in w_planes:
            copy.wait_send()

    def drain(p, carry):
        @pl.when(c == 0)
        def _():
            term_copy(p).wait_send()

        @pl.when(c == 1)
        def _():
            @pl.when(y == 0)
            def _():
                sum_up(p).wait_send()
                sum_wrap(p).wait_send()

            @pl.when(jnp.logical_or(y == 1, y == 2))
            def _():
                sum_next(p).wait_send()

            @pl.when(y == 3)
            def _():
                pass_down(p).wait_send()

            @pl.when(y > 0)
            def _():
                back_in0(p).wait_send()
        return carry

    lax.fori_loop(0, PIECES, drain, 0)


def sweep(ids, sched, window, x, w, ae, md, mu):
    vm = pl.BlockSpec(memory_space=pltpu.VMEM)
    sm = pl.BlockSpec(memory_space=pltpu.SMEM)
    anywhere = pl.BlockSpec(memory_space=pl.ANY)
    dma = pltpu.SemaphoreType.DMA
    return pl.pallas_call(
        sweep_kernel,
        out_shape=(
            jax.ShapeDtypeStruct((256, 2048), BF16), jax.ShapeDtypeStruct((256, 2048), BF16),
            jax.ShapeDtypeStruct((1, 2048), F32), jax.ShapeDtypeStruct((1, 128), F32),
        ),
        in_specs=[sm, sm, sm, vm, anywhere, anywhere, anywhere, anywhere],
        out_specs=(vm, vm, vm, vm),
        scratch_shapes=[
            pltpu.VMEM((16, 256, 2048), BF16),
            pltpu.VMEM((2048, 384), BF16),
            pltpu.VMEM((2048, 384), BF16),
            pltpu.VMEM((1, 384), F32),
            pltpu.VMEM((512, 2048), BF16),
            pltpu.VMEM((2048, 256), BF16),
            pltpu.VMEM((256, 6144), BF16),
            pltpu.VMEM((16, 256, 256), BF16),
            pltpu.VMEM((16, 256, 256), BF16),
            pltpu.VMEM((16, 256, 256), F32),
            pltpu.VMEM((PIECES, 16, PIECE, 128), BF16),
            pltpu.VMEM((256, 2048), BF16),
            pltpu.VMEM((1, 2048), F32),
            pltpu.VMEM((256, 2048), BF16),
            pltpu.VMEM((256, 2048), BF16),
            pltpu.VMEM((256, 2048), BF16),
            pltpu.VMEM((256, 2048), BF16),
            dma((4,)), dma((2,)), dma((2,)), dma((2,)), dma, dma((16,)), dma((16,)), dma((4,)), dma((4,)),
            dma((17,)), dma((17,)), dma, dma((PIECES,)),
            *[dma((PIECES,)) for _ in range(8)],
        ],
        compiler_params=pltpu.CompilerParams(
            collective_id=1, has_side_effects=True, vmem_limit_bytes=60 * 1024 * 1024
        ),
    )(ids, sched, window, x, w, ae, md, mu)


def on_device(
    iterate,
    query_key_value_weight,
    modulation_down_weight,
    modulation_up_weight,
    action_embedding_matrix,
    action_token_index,
    sched,
    window,
):
    rows = iterate[0]
    mixed, earlier, gate, delta = sweep(
        action_token_index,
        sched,
        window,
        rows,
        query_key_value_weight[:, 0],
        action_embedding_matrix,
        modulation_down_weight,
        modulation_up_weight,
    )
    velocity = gate * mixed.astype(F32)
    entering = jnp.where(lax.axis_index("step") == 0, rows, earlier.astype(F32))
    new_states = entering + delta[:, :1] * velocity
    return (new_states[None], velocity[None])


def solution(mesh):
    placed = (P("step", "seq", None), P(None, "seq", None), P(), P(), P(), P(), P(), P())
    return jax.shard_map(
        on_device,
        mesh=mesh,
        in_specs=placed,
        out_specs=(P("step", "seq", None), P("step", "seq", None)),
        check_vma=False,
    )
```

```python
import math

import jax
import jax.numpy as jnp
from jax import lax
from jax.experimental import pallas as pl
from jax.experimental.pallas import tpu as pltpu
from jax.sharding import PartitionSpec as P

MESH = pl.DeviceIdType.MESH
F32, BF16 = jnp.float32, jnp.bfloat16
PIECES = 8
REST = ((0, 8, 8), (8, 11, 11), (11, 14, 14), (14, 16, 16))
LAGS = ((3, "begin"), (5, "middle"), (7, "end"))
PIECE = 256 // PIECES
GROUPS = ((0, 1, 12, 4, 2), (3, 5, 13), (6, 8, 9), (14, 15, 7), (10, 11))
ORDER = sum(GROUPS, ())
FACTOR = 2.5 / math.sqrt(128) * math.log2(math.e)


def remote(src, dst, send, recv, device):
    return pltpu.make_async_remote_copy(
        src_ref=src, dst_ref=dst, send_sem=send, recv_sem=recv, device_id=device, device_id_type=MESH
    )


def inverse_rms(value):
    return lax.rsqrt(jnp.mean(value * value, axis=-1, keepdims=True) + 1e-6)


def sweep_kernel(
    ids, sched, window, x_hbm, w_ref, ae_ref, md_ref, mu_ref,
    new_ref, vel_ref,
    mixed, pin, new, vel, x_ref, gate_row,
    xbuf, wraw, wmod, bias, ae, md, mu, qk, v1, acc, ostage, pout, gd, sout, tin, in0, in1,
    load_sem, home_s, home_r, guest_s, guest_r, share_s, share_r, wx_s, wx_r,
    hop_s, hop_r, out_s, out_r, t_s, t_r, s0_s, s0_r, s1_s, s1_r, e_s, e_r, put_sem,
):
    step, seq = lax.axis_index("step"), lax.axis_index("seq")
    y, c = step // 2, lax.rem(step, 2)
    z, x = seq // 4, lax.rem(seq, 4)
    m = x // 2
    stays = c == m
    head = jnp.where(c == 0, seq, z * 4 + 3 - x)

    def device(core, dz, column):
        return (y * 2 + core, lax.rem(z + dz + 4, 4) * 4 + column)

    x_load = pltpu.make_async_copy(x_hbm, x_ref, load_sem.at[4])
    x_load.start()
    mate = device(c, 0, x + 1 - 2 * lax.rem(x, 2))
    up, down = device(c, 1, x), device(c, -1, x)
    sibling = device(1 - c, 0, x)
    across = [device(core, 0, 3 - x) for core in range(2)]
    planes = [(lax.rem(y + dy, 4) * 2 + c, seq) for dy in (1, 3, 2)]

    barrier = pltpu.get_barrier_semaphore()
    for other in (mate, up, down, sibling, *across, *planes):
        pl.semaphore_signal(barrier, inc=1, device_id=other, device_id_type=MESH)
    for other_z in range(4):
        for column in range(2):
            for core in range(2):
                source = (y * 2 + core, other_z * 4 + 2 * c + column)
                itself = jnp.logical_and(core == c, other_z * 4 + 2 * c + column == seq)

                @pl.when(jnp.logical_not(itself))
                def _():
                    pl.semaphore_signal(barrier, inc=1, device_id=source, device_id_type=MESH)

    loads = [
        pltpu.make_async_copy(ae_ref, ae, load_sem.at[0]),
        pltpu.make_async_copy(md_ref, md, load_sem.at[1]),
        pltpu.make_async_copy(mu_ref, mu, load_sem.at[2]),
    ]
    for load in loads:
        load.start()
    own_w = pltpu.make_async_copy(w_ref, wraw, load_sem.at[3])

    @pl.when(c == 0)
    def _():
        own_w.start()

    mine = pl.ds(pl.multiple_of(c * 128, 128), 128)
    theirs = pl.ds(pl.multiple_of((1 - c) * 128, 128), 128)

    home_out = [
        remote(xbuf.at[0, theirs], xbuf.at[0, theirs], home_s.at[0], home_r.at[0], sibling),
        remote(xbuf.at[0, mine], xbuf.at[0, mine], home_s.at[1], home_r.at[1], sibling),
    ]
    guest_out = [
        remote(pout.at[pl.ds(core * 128, 128)], xbuf.at[1, pl.ds(core * 128, 128)], guest_s.at[core], guest_r, across[core])
        for core in range(2)
    ]

    pl.semaphore_wait(barrier, 9 + 16 - stays.astype(jnp.int32))

    quarter = pl.ds(pl.multiple_of(y * 512, 512), 512)
    w_across = remote(w_ref.at[quarter], wraw.at[quarter], wx_s.at[0], wx_r.at[0], across[1])
    w_planes = [
        remote(wraw.at[quarter], wraw.at[quarter], wx_s.at[i + 1], wx_r.at[i + 1], planes[i]) for i in range(3)
    ]

    @pl.when(c == 1)
    def _():
        w_across.start()

    x_load.wait()
    value = x_ref[...]
    unit = (value * inverse_rms(value)).astype(BF16)

    @pl.when(stays)
    def _():
        xbuf[0] = unit
        home_out[0].start()

    @pl.when(jnp.logical_not(stays))
    def _():
        pout[...] = unit
        for copy in guest_out:
            copy.start()
        home_out[0].wait_recv()

    hops = []

    def hop(index, slot, to, to_slot, first=0, count=128):
        rows = pl.ds(pl.multiple_of(c * 128 + first, 32), count)
        copy = remote(xbuf.at[slot, rows], xbuf.at[to_slot, rows], hop_s.at[index], hop_r.at[index], to)
        hops.append(copy)
        return copy

    shares = {}

    def share(slot):
        shares[slot] = remote(xbuf.at[slot, mine], xbuf.at[slot, mine], share_s.at[slot], share_r.at[slot], sibling)
        shares[slot].start()

    h01 = hop(0, 0, mate, 2)
    h30 = hop(1, 0, up, 12)
    h10 = hop(2, 0, down, 4)
    for copy in (h01, h30, h10):
        copy.start()

    @pl.when(stays)
    def _():
        home_out[1].start()

    stamps = [sched[window[2 * y + i]].astype(F32) for i in range(3)]
    row8 = lax.broadcasted_iota(jnp.int32, (8, 1024), 0)
    lane = lax.broadcasted_iota(jnp.int32, (8, 1024), 1).astype(F32)
    angles = jnp.where(row8 == 0, stamps[0], stamps[1]) * jnp.exp(-math.log(10000.0) / 1024 * lane)
    temb = jnp.concatenate([jnp.cos(angles), jnp.sin(angles)], axis=1)
    vocab = lax.broadcasted_iota(jnp.int32, (16, 512), 1)
    counts = jnp.zeros((16, 512), F32)
    for i in range(12):
        counts += (vocab == ids[i]).astype(F32)
    for load in loads:
        load.wait()
    mean = jnp.dot(counts.astype(BF16), ae[...], preferred_element_type=F32)[:8] / 12.0
    cond = temb + mean
    cond = (cond / (1.0 + jnp.exp(-cond))).astype(BF16)
    low = jnp.dot(cond, md[...], preferred_element_type=F32).astype(BF16)
    factors = jnp.dot(low, mu[...], preferred_element_type=F32)
    scale_cols = lax.dot_general(
        mu[:, 2048:4096], low, (((0,), (1,)), ((), ())), preferred_element_type=F32
    )
    rows = lax.broadcasted_iota(jnp.int32, (8, 2048), 0)
    gate = jnp.sum(jnp.where(rows == c, factors[:, 4096:], 0.0), axis=0, keepdims=True)
    delta = jnp.where(c == 0, stamps[1] / 1000.0 - stamps[0] / 1000.0, stamps[2] / 1000.0 - stamps[1] / 1000.0)
    gate_row[...] = gate
    gd[...] = gate * delta
    columns = lax.broadcasted_iota(jnp.int32, (2048, 8), 1)
    scale = jnp.sum(jnp.where(columns == m, scale_cols, 0.0), axis=1, keepdims=True)
    shift = factors[:, :2048]
    shift_high = shift.astype(BF16)
    shift_low = (shift - shift_high.astype(F32)).astype(BF16)

    @pl.when(c == 1)
    def _():
        w_across.wait_recv()
        for copy in w_planes:
            copy.start()

    guest_out[0].wait_recv()
    g01, g30, g10 = hop(3, 1, mate, 3), hop(4, 1, up, 13), hop(5, 1, down, 5)
    for copy in (g01, g30, g10):
        copy.start()
    share(1)
    h30.wait_recv()
    h20, x31h = hop(6, 12, up, 8), hop(7, 12, mate, 14)
    h20.start()
    x31h.start()
    share(12)
    h10.wait_recv()
    x11h = hop(8, 4, mate, 6)
    x11h.start()
    share(4)
    h01.wait_recv()
    share(2)

    g01.wait_recv()
    g31, g11 = hop(9, 3, up, 15), hop(10, 3, down, 7)
    g31.start()
    g11.start()
    share(3)
    g10.wait_recv()
    g20 = hop(11, 5, down, 9)
    g20.start()
    share(5)
    g30.wait_recv()
    share(13)

    @pl.when(c == 0)
    def _():
        own_w.wait()

    @pl.when(c == 1)
    def _():
        for copy in w_planes:
            copy.wait_recv()

    for i in range(4):
        part = pl.ds(i * 512, 512)
        wmod[part] = (wraw[part].astype(F32) * (1.0 + scale[i * 512:(i + 1) * 512])).astype(BF16)
    shifted = jnp.dot(shift_high, wraw[...], preferred_element_type=F32)
    shifted += jnp.dot(shift_low, wraw[...], preferred_element_type=F32)
    rows = lax.broadcasted_iota(jnp.int32, (8, 384), 0)
    bias[...] = jnp.sum(jnp.where(rows == m, shifted, 0.0), axis=0, keepdims=True)
    v1[:, :, 128:] = jnp.ones((16, 256, 128), BF16)

    def block_of(slot):
        zr, kind = slot // 4, slot % 4
        other = x + 1 - 2 * lax.rem(x, 2)
        return lax.rem(z + zr, 4) * 4 + (x, 3 - x, other, 3 - other)[kind]

    def project(slot):
        place = ORDER.index(slot)
        p = jnp.dot(xbuf[slot], wmod[...], preferred_element_type=F32) + bias[...]
        q, k = p[:, :128], p[:, 128:256]
        qk[place, :, :128] = (q * (inverse_rms(q) * FACTOR)).astype(BF16)
        qk[place, :, 128:] = (k * inverse_rms(k)).astype(BF16)
        v1[place, :, :128] = p[:, 256:].astype(BF16)

    def weigh(q, first, last):
        keys = qk[first:last, :, 128:].reshape((last - first) * 256, 128)
        values = v1[first:last].reshape((last - first) * 256, 256)
        s = lax.dot_general(q, keys, (((1,), (1,)), ((), ())), preferred_element_type=F32)
        return jnp.dot(jnp.exp2(s).astype(BF16), values, preferred_element_type=F32)

    def fresh(first, last):
        count = last - first
        q = qk[first:last, :, :128].reshape(count * 256, 128)
        for at in range(0, last, 4):
            part = weigh(q, at, min(at + 4, last)).reshape(count, 256, 256)
            if at == 0:
                acc[first:last] = part
            else:
                acc[first:last] += part

    def extend(first, last):
        for half in range(2):
            rows = pl.ds(half * 128, 128)
            q = qk[:first, rows, :128].reshape(first * 128, 128)
            acc[:first, rows] += weigh(q, first, last).reshape(first, 128, 256)

    def absorb(group):
        first = ORDER.index(GROUPS[group][0])
        last = first + len(GROUPS[group])
        for slot in GROUPS[group]:
            if slot:
                shares[slot].wait_recv()
            else:
                @pl.when(jnp.logical_not(stays))
                def _():
                    home_out[1].wait_recv()
            project(slot)
        if 0 < group < 2:
            extend(first, last)
        fresh(first, last)

    absorb(0)
    absorb(1)
    x11h.wait_recv()
    part11 = hop(12, 6, down, 10, 32, 32)
    part11.start()
    share(6)
    h20.wait_recv()
    part20 = hop(13, 8, mate, 10, 64, 64)
    part20.start()
    share(8)
    g20.wait_recv()
    share(9)
    x31h.wait_recv()
    part31 = hop(14, 14, up, 10, 0, 32)
    part31.start()
    share(14)
    g31.wait_recv()
    part31g = hop(15, 15, up, 11, 0, 64)
    part31g.start()
    share(15)
    g11.wait_recv()
    part11g = hop(16, 7, down, 11, 64, 64)
    part11g.start()
    share(7)
    absorb(2)
    absorb(3)
    part31.wait_recv()
    part11.wait_recv()
    part20.wait_recv()
    share(10)
    part31g.wait_recv()
    part11g.wait_recv()
    share(11)
    absorb(4)

    @pl.when(jnp.logical_not(stays))
    def _():
        for copy in guest_out:
            copy.wait_send()


    own_columns = pl.ds(pl.multiple_of(head * 128, 128), 128)
    dests = [block_of(slot) for slot in ORDER]

    def rows_of(p):
        return pl.ds(pl.multiple_of(p * PIECE, PIECE), PIECE)

    def out_copy(p, place):
        return remote(
            ostage.at[p, place], mixed.at[rows_of(p), own_columns], out_s, out_r.at[p], (y * 2 + m, dests[place])
        )

    def keep_copy(p):
        return pltpu.make_async_copy(ostage.at[p, 0], mixed.at[rows_of(p), own_columns], out_r.at[p])

    def finish(p):
        rows = rows_of(p)
        for first, last, done in REST:
            count = last - first
            total = acc[first:last, rows].reshape(count * PIECE, 256)
            q = qk[first:last, rows, :128].reshape(count * PIECE, 128)
            for at in range(done, 16, 4):
                total += weigh(q, at, min(at + 4, 16))
            ostage[p, first:last] = (total[:, :128] / total[:, 128:]).astype(BF16).reshape(count, PIECE, 128)

        @pl.when(stays)
        def _():
            keep_copy(p).start()

        @pl.when(jnp.logical_not(stays))
        def _():
            out_copy(p, 0).start()

        for place in range(1, 16):
            out_copy(p, place).start()

    def hand(src, dst, send, recv, p, to):
        return remote(src.at[rows_of(p)], dst.at[rows_of(p)], send.at[p], recv.at[p], to)

    above, below, _ = planes
    term_copy = lambda p: hand(pout, tin, t_s, t_r, p, sibling)
    sum_up = lambda p: hand(sout, in0, s0_s, s0_r, p, above)
    sum_wrap = lambda p: hand(sout, in0, s1_s, s0_r, p, below)
    sum_next = lambda p: hand(sout, in1, s1_s, s1_r, p, above)
    pass_down = lambda p: hand(in0, in0, s0_s, s0_r, p, below)
    back_in0 = lambda p: hand(in0, pin, e_s, e_r, p, sibling)
    back_pout = lambda p: hand(pout, pin, e_s, e_r, p, sibling)

    def load(ref, p):
        return ref[rows_of(p)].astype(F32)

    def begin(p):
        rows = rows_of(p)
        pltpu.make_async_copy(mixed.at[rows], mixed.at[rows], out_r.at[p]).wait()
        here = load(mixed, p)
        term = gd[...] * here
        vel[rows] = gate_row[...] * here
        pltpu.make_async_copy(vel.at[rows], vel_ref.at[rows], put_sem.at[0]).start()

        @pl.when(c == 0)
        def _():
            @pl.when(y == 0)
            def _():
                pout[rows] = (x_ref[rows] + term).astype(BF16)

            @pl.when(y > 0)
            def _():
                pout[rows] = term.astype(BF16)

            term_copy(p).start()

        @pl.when(c == 1)
        def _():
            term_copy(p).wait_recv()

            @pl.when(y < 2)
            def _():
                sout[rows] = (load(tin, p) + term).astype(BF16)

            @pl.when(y == 0)
            def _():
                sum_up(p).start()
                sum_wrap(p).start()

            @pl.when(y == 1)
            def _():
                sum_next(p).start()

            @pl.when(y == 2)
            def _():
                sout[rows] = (load(tin, p) + term).astype(BF16)

    def middle(p):
        rows = rows_of(p)

        @pl.when(jnp.logical_and(c == 1, y == 2))
        def _():
            sum_next(p).wait_recv()
            sout[rows] = (load(in1, p) + load(sout, p)).astype(BF16)
            sum_next(p).start()

        @pl.when(jnp.logical_and(c == 1, y == 3))
        def _():
            sum_up(p).wait_recv()
            pass_down(p).start()

    def end(p):
        rows = rows_of(p)

        term = gd[...] * load(mixed, p)

        @pl.when(step == 0)
        def _():
            new[rows] = x_ref[rows] + term

        @pl.when(jnp.logical_and(c == 0, y > 0))
        def _():
            back_in0(p).wait_recv()
            new[rows] = load(pin, p) + term

        @pl.when(jnp.logical_and(c == 1, y == 0))
        def _():
            new[rows] = load(tin, p) + term

        @pl.when(jnp.logical_and(c == 1, y == 1))
        def _():
            sum_up(p).wait_recv()
            back_in0(p).start()
            new[rows] = load(in0, p) + load(tin, p) + term

        @pl.when(jnp.logical_and(c == 1, y > 1))
        def _():
            @pl.when(y == 2)
            def _():
                pass_down(p).wait_recv()

            @pl.when(y == 3)
            def _():
                sum_next(p).wait_recv()

            total = load(in0, p) + load(in1, p)
            pout[rows] = total.astype(BF16)
            back_pout(p).start()
            new[rows] = total + load(tin, p) + term

        pltpu.make_async_copy(new.at[rows], new_ref.at[rows], put_sem.at[1]).start()

    def body(p, carry):
        @pl.when(p < PIECES)
        def _():
            finish(p)

        for lag, part in LAGS:
            @pl.when(jnp.logical_and(p >= lag, p < PIECES + lag))
            def _(lag=lag, part=part):
                stages[part](p - lag)
        return carry

    stages = {"begin": begin, "middle": middle, "end": end}
    lax.fori_loop(0, PIECES + LAGS[-1][0], body, 0)

    for copy in hops:
        copy.wait_send()
    for slot in shares:
        shares[slot].wait_send()

    @pl.when(stays)
    def _():
        for copy in home_out:
            copy.wait_send()
        pltpu.make_async_copy(ostage.at[:, 1:], ostage.at[:, 1:], out_s).wait()

    @pl.when(jnp.logical_not(stays))
    def _():
        pltpu.make_async_copy(ostage, ostage, out_s).wait()

    @pl.when(c == 1)
    def _():
        w_across.wait_send()
        for copy in w_planes:
            copy.wait_send()

    def drain(p, carry):
        @pl.when(c == 0)
        def _():
            term_copy(p).wait_send()

        @pl.when(c == 1)
        def _():
            @pl.when(y == 0)
            def _():
                sum_up(p).wait_send()
                sum_wrap(p).wait_send()

            @pl.when(jnp.logical_or(y == 1, y == 2))
            def _():
                sum_next(p).wait_send()

            @pl.when(y == 3)
            def _():
                pass_down(p).wait_send()

            @pl.when(y > 0)
            def _():
                back_in0(p).wait_send()
        return carry

    lax.fori_loop(0, PIECES, drain, 0)
    pltpu.make_async_copy(vel, vel_ref, put_sem.at[0]).wait()
    pltpu.make_async_copy(new, new_ref, put_sem.at[1]).wait()


def sweep(ids, sched, window, x, w, ae, md, mu):
    sm = pl.BlockSpec(memory_space=pltpu.SMEM)
    anywhere = pl.BlockSpec(memory_space=pl.ANY)
    dma = pltpu.SemaphoreType.DMA
    return pl.pallas_call(
        sweep_kernel,
        out_shape=(
            jax.ShapeDtypeStruct((256, 2048), F32), jax.ShapeDtypeStruct((256, 2048), F32),
        ),
        in_specs=[sm, sm, sm, anywhere, anywhere, anywhere, anywhere, anywhere],
        out_specs=(anywhere, anywhere),
        scratch_shapes=[
            pltpu.VMEM((256, 2048), BF16),
            pltpu.VMEM((256, 2048), BF16),
            pltpu.VMEM((256, 2048), F32),
            pltpu.VMEM((256, 2048), F32),
            pltpu.VMEM((256, 2048), F32),
            pltpu.VMEM((1, 2048), F32),
            pltpu.VMEM((16, 256, 2048), BF16),
            pltpu.VMEM((2048, 384), BF16),
            pltpu.VMEM((2048, 384), BF16),
            pltpu.VMEM((1, 384), F32),
            pltpu.VMEM((512, 2048), BF16),
            pltpu.VMEM((2048, 256), BF16),
            pltpu.VMEM((256, 6144), BF16),
            pltpu.VMEM((16, 256, 256), BF16),
            pltpu.VMEM((16, 256, 256), BF16),
            pltpu.VMEM((16, 256, 256), F32),
            pltpu.VMEM((PIECES, 16, PIECE, 128), BF16),
            pltpu.VMEM((256, 2048), BF16),
            pltpu.VMEM((1, 2048), F32),
            pltpu.VMEM((256, 2048), BF16),
            pltpu.VMEM((256, 2048), BF16),
            pltpu.VMEM((256, 2048), BF16),
            pltpu.VMEM((256, 2048), BF16),
            dma((5,)), dma((2,)), dma((2,)), dma((2,)), dma, dma((16,)), dma((16,)), dma((4,)), dma((4,)),
            dma((17,)), dma((17,)), dma, dma((PIECES,)),
            *[dma((PIECES,)) for _ in range(8)], dma((2,)),
        ],
        compiler_params=pltpu.CompilerParams(
            collective_id=1, has_side_effects=True, vmem_limit_bytes=60 * 1024 * 1024
        ),
    )(ids, sched, window, x, w, ae, md, mu)


def on_device(
    iterate,
    query_key_value_weight,
    modulation_down_weight,
    modulation_up_weight,
    action_embedding_matrix,
    action_token_index,
    sched,
    window,
):
    new_states, velocity = sweep(
        action_token_index,
        sched,
        window,
        iterate[0],
        query_key_value_weight[:, 0],
        action_embedding_matrix,
        modulation_down_weight,
        modulation_up_weight,
    )
    return (new_states[None], velocity[None])


def solution(mesh):
    placed = (P("step", "seq", None), P(None, "seq", None), P(), P(), P(), P(), P(), P())
    return jax.shard_map(
        on_device,
        mesh=mesh,
        in_specs=placed,
        out_specs=(P("step", "seq", None), P("step", "seq", None)),
        check_vma=False,
    )
```

```python
import math

import jax
import jax.numpy as jnp
from jax import lax
from jax.experimental import pallas as pl
from jax.experimental.pallas import tpu as pltpu
from jax.sharding import PartitionSpec as P

MESH = pl.DeviceIdType.MESH
F32, BF16 = jnp.float32, jnp.bfloat16
PIECES = 8
REST = ((0, 16, 8),)
LAGS = ((3, "begin"), (5, "middle"), (7, "end"))
PIECE = 256 // PIECES
GROUPS = ((0, 1, 12, 4, 2), (3, 5, 13), (6, 8, 9), (14, 15, 7), (10, 11))
ORDER = sum(GROUPS, ())
FACTOR = 2.5 / math.sqrt(128) * math.log2(math.e)


def remote(src, dst, send, recv, device):
    return pltpu.make_async_remote_copy(
        src_ref=src, dst_ref=dst, send_sem=send, recv_sem=recv, device_id=device, device_id_type=MESH
    )


def inverse_rms(value):
    return lax.rsqrt(jnp.mean(value * value, axis=-1, keepdims=True) + 1e-6)


def sweep_kernel(
    ids, sched, window, x_hbm, w_ref, ae_ref, md_ref, mu_ref,
    new_ref, vel_ref,
    mixed, pin, new, vel, x_ref, gate_row,
    xbuf, wraw, wmod, bias, ae, md, mu, qk, v1, acc, ostage, pout, gd, sout, tin, in0, in1,
    load_sem, home_s, home_r, guest_s, guest_r, share_s, share_r, wx_s, wx_r,
    hop_s, hop_r, out_s, out_r, t_s, t_r, s0_s, s0_r, s1_s, s1_r, e_s, e_r, put_sem,
):
    step, seq = lax.axis_index("step"), lax.axis_index("seq")
    y, c = step // 2, lax.rem(step, 2)
    z, x = seq // 4, lax.rem(seq, 4)
    m = x // 2
    stays = c == m
    head = jnp.where(c == 0, seq, z * 4 + 3 - x)

    def device(core, dz, column):
        return (y * 2 + core, lax.rem(z + dz + 4, 4) * 4 + column)

    x_load = pltpu.make_async_copy(x_hbm, x_ref, load_sem.at[4])
    x_load.start()
    mate = device(c, 0, x + 1 - 2 * lax.rem(x, 2))
    up, down = device(c, 1, x), device(c, -1, x)
    sibling = device(1 - c, 0, x)
    across = [device(core, 0, 3 - x) for core in range(2)]
    planes = [(lax.rem(y + dy, 4) * 2 + c, seq) for dy in (1, 3, 2)]

    barrier = pltpu.get_barrier_semaphore()
    for other in (mate, up, down, sibling, *across, *planes):
        pl.semaphore_signal(barrier, inc=1, device_id=other, device_id_type=MESH)
    for other_z in range(4):
        for column in range(2):
            for core in range(2):
                source = (y * 2 + core, other_z * 4 + 2 * c + column)
                itself = jnp.logical_and(core == c, other_z * 4 + 2 * c + column == seq)

                @pl.when(jnp.logical_not(itself))
                def _():
                    pl.semaphore_signal(barrier, inc=1, device_id=source, device_id_type=MESH)

    loads = [
        pltpu.make_async_copy(ae_ref, ae, load_sem.at[0]),
        pltpu.make_async_copy(md_ref, md, load_sem.at[1]),
        pltpu.make_async_copy(mu_ref, mu, load_sem.at[2]),
    ]
    for load in loads:
        load.start()
    own_w = pltpu.make_async_copy(w_ref, wraw, load_sem.at[3])

    @pl.when(c == 0)
    def _():
        own_w.start()

    mine = pl.ds(pl.multiple_of(c * 128, 128), 128)
    theirs = pl.ds(pl.multiple_of((1 - c) * 128, 128), 128)

    home_out = [
        remote(xbuf.at[0, theirs], xbuf.at[0, theirs], home_s.at[0], home_r.at[0], sibling),
        remote(xbuf.at[0, mine], xbuf.at[0, mine], home_s.at[1], home_r.at[1], sibling),
    ]
    guest_out = [
        remote(pout.at[pl.ds(core * 128, 128)], xbuf.at[1, pl.ds(core * 128, 128)], guest_s.at[core], guest_r, across[core])
        for core in range(2)
    ]

    pl.semaphore_wait(barrier, 9 + 16 - stays.astype(jnp.int32))

    quarter = pl.ds(pl.multiple_of(y * 512, 512), 512)
    w_across = remote(w_ref.at[quarter], wraw.at[quarter], wx_s.at[0], wx_r.at[0], across[1])
    w_planes = [
        remote(wraw.at[quarter], wraw.at[quarter], wx_s.at[i + 1], wx_r.at[i + 1], planes[i]) for i in range(3)
    ]

    @pl.when(c == 1)
    def _():
        w_across.start()

    x_load.wait()
    value = x_ref[...]
    unit = (value * inverse_rms(value)).astype(BF16)

    @pl.when(stays)
    def _():
        xbuf[0] = unit
        home_out[0].start()

    @pl.when(jnp.logical_not(stays))
    def _():
        pout[...] = unit
        for copy in guest_out:
            copy.start()
        home_out[0].wait_recv()

    hops = []

    def hop(index, slot, to, to_slot, first=0, count=128):
        rows = pl.ds(pl.multiple_of(c * 128 + first, 32), count)
        copy = remote(xbuf.at[slot, rows], xbuf.at[to_slot, rows], hop_s.at[index], hop_r.at[index], to)
        hops.append(copy)
        return copy

    shares = {}

    def share(slot):
        shares[slot] = remote(xbuf.at[slot, mine], xbuf.at[slot, mine], share_s.at[slot], share_r.at[slot], sibling)
        shares[slot].start()

    h01 = hop(0, 0, mate, 2)
    h30 = hop(1, 0, up, 12)
    h10 = hop(2, 0, down, 4)
    for copy in (h01, h30, h10):
        copy.start()

    @pl.when(stays)
    def _():
        home_out[1].start()

    stamps = [sched[window[2 * y + i]].astype(F32) for i in range(3)]
    row8 = lax.broadcasted_iota(jnp.int32, (8, 1024), 0)
    lane = lax.broadcasted_iota(jnp.int32, (8, 1024), 1).astype(F32)
    angles = jnp.where(row8 == 0, stamps[0], stamps[1]) * jnp.exp(-math.log(10000.0) / 1024 * lane)
    temb = jnp.concatenate([jnp.cos(angles), jnp.sin(angles)], axis=1)
    vocab = lax.broadcasted_iota(jnp.int32, (16, 512), 1)
    counts = jnp.zeros((16, 512), F32)
    for i in range(12):
        counts += (vocab == ids[i]).astype(F32)
    for load in loads:
        load.wait()
    mean = jnp.dot(counts.astype(BF16), ae[...], preferred_element_type=F32)[:8] / 12.0
    cond = temb + mean
    cond = (cond / (1.0 + jnp.exp(-cond))).astype(BF16)
    low = jnp.dot(cond, md[...], preferred_element_type=F32).astype(BF16)
    factors = jnp.dot(low, mu[...], preferred_element_type=F32)
    scale_cols = lax.dot_general(
        mu[:, 2048:4096], low, (((0,), (1,)), ((), ())), preferred_element_type=F32
    )
    rows = lax.broadcasted_iota(jnp.int32, (8, 2048), 0)
    gate = jnp.sum(jnp.where(rows == c, factors[:, 4096:], 0.0), axis=0, keepdims=True)
    delta = jnp.where(c == 0, stamps[1] / 1000.0 - stamps[0] / 1000.0, stamps[2] / 1000.0 - stamps[1] / 1000.0)
    gate_row[...] = gate
    gd[...] = gate * delta
    columns = lax.broadcasted_iota(jnp.int32, (2048, 8), 1)
    scale = jnp.sum(jnp.where(columns == m, scale_cols, 0.0), axis=1, keepdims=True)
    shift = factors[:, :2048]
    shift_high = shift.astype(BF16)
    shift_low = (shift - shift_high.astype(F32)).astype(BF16)

    @pl.when(c == 1)
    def _():
        w_across.wait_recv()
        for copy in w_planes:
            copy.start()

    guest_out[0].wait_recv()
    g01, g30, g10 = hop(3, 1, mate, 3), hop(4, 1, up, 13), hop(5, 1, down, 5)
    for copy in (g01, g30, g10):
        copy.start()
    share(1)
    h30.wait_recv()
    h20, x31h = hop(6, 12, up, 8), hop(7, 12, mate, 14)
    h20.start()
    x31h.start()
    share(12)
    h10.wait_recv()
    x11h = hop(8, 4, mate, 6)
    x11h.start()
    share(4)
    h01.wait_recv()
    share(2)

    g01.wait_recv()
    g31, g11 = hop(9, 3, up, 15), hop(10, 3, down, 7)
    g31.start()
    g11.start()
    share(3)
    g10.wait_recv()
    g20 = hop(11, 5, down, 9)
    g20.start()
    share(5)
    g30.wait_recv()
    share(13)

    @pl.when(c == 0)
    def _():
        own_w.wait()

    @pl.when(c == 1)
    def _():
        for copy in w_planes:
            copy.wait_recv()

    for i in range(4):
        part = pl.ds(i * 512, 512)
        wmod[part] = (wraw[part].astype(F32) * (1.0 + scale[i * 512:(i + 1) * 512])).astype(BF16)
    shifted = jnp.dot(shift_high, wraw[...], preferred_element_type=F32)
    shifted += jnp.dot(shift_low, wraw[...], preferred_element_type=F32)
    rows = lax.broadcasted_iota(jnp.int32, (8, 384), 0)
    bias[...] = jnp.sum(jnp.where(rows == m, shifted, 0.0), axis=0, keepdims=True)
    v1[:, :, 128:] = jnp.ones((16, 256, 128), BF16)

    def block_of(slot):
        zr, kind = slot // 4, slot % 4
        other = x + 1 - 2 * lax.rem(x, 2)
        return lax.rem(z + zr, 4) * 4 + (x, 3 - x, other, 3 - other)[kind]

    def project(slot):
        place = ORDER.index(slot)
        p = jnp.dot(xbuf[slot], wmod[...], preferred_element_type=F32) + bias[...]
        q, k = p[:, :128], p[:, 128:256]
        qk[place, :, :128] = (q * (inverse_rms(q) * FACTOR)).astype(BF16)
        qk[place, :, 128:] = (k * inverse_rms(k)).astype(BF16)
        v1[place, :, :128] = p[:, 256:].astype(BF16)

    def weigh(q, first, last):
        keys = qk[first:last, :, 128:].reshape((last - first) * 256, 128)
        values = v1[first:last].reshape((last - first) * 256, 256)
        s = lax.dot_general(q, keys, (((1,), (1,)), ((), ())), preferred_element_type=F32)
        return jnp.dot(jnp.exp2(s).astype(BF16), values, preferred_element_type=F32)

    def fresh(first, last):
        count = last - first
        q = qk[first:last, :, :128].reshape(count * 256, 128)
        for at in range(0, min(last, 8), 4):
            part = weigh(q, at, min(at + 4, last)).reshape(count, 256, 256)
            if at == 0:
                acc[first:last] = part
            else:
                acc[first:last] += part

    def extend(first, last):
        for half in range(2):
            rows = pl.ds(half * 128, 128)
            q = qk[:first, rows, :128].reshape(first * 128, 128)
            acc[:first, rows] += weigh(q, first, last).reshape(first, 128, 256)

    def absorb(group):
        first = ORDER.index(GROUPS[group][0])
        last = first + len(GROUPS[group])
        for slot in GROUPS[group]:
            if slot:
                shares[slot].wait_recv()
            else:
                @pl.when(jnp.logical_not(stays))
                def _():
                    home_out[1].wait_recv()
            project(slot)
        if 0 < group < 2:
            extend(first, last)
        fresh(first, last)

    absorb(0)
    absorb(1)
    x11h.wait_recv()
    part11 = hop(12, 6, down, 10, 32, 32)
    part11.start()
    share(6)
    h20.wait_recv()
    part20 = hop(13, 8, mate, 10, 64, 64)
    part20.start()
    share(8)
    g20.wait_recv()
    share(9)
    x31h.wait_recv()
    part31 = hop(14, 14, up, 10, 0, 32)
    part31.start()
    share(14)
    g31.wait_recv()
    part31g = hop(15, 15, up, 11, 0, 64)
    part31g.start()
    share(15)
    g11.wait_recv()
    part11g = hop(16, 7, down, 11, 64, 64)
    part11g.start()
    share(7)
    absorb(2)
    absorb(3)
    part31.wait_recv()
    part11.wait_recv()
    part20.wait_recv()
    share(10)
    part31g.wait_recv()
    part11g.wait_recv()
    share(11)
    absorb(4)

    @pl.when(jnp.logical_not(stays))
    def _():
        for copy in guest_out:
            copy.wait_send()


    own_columns = pl.ds(pl.multiple_of(head * 128, 128), 128)
    dests = [block_of(slot) for slot in ORDER]

    def rows_of(p):
        return pl.ds(pl.multiple_of(p * PIECE, PIECE), PIECE)

    def out_copy(p, place):
        return remote(
            ostage.at[p, place], mixed.at[rows_of(p), own_columns], out_s, out_r.at[p], (y * 2 + m, dests[place])
        )

    def keep_copy(p):
        return pltpu.make_async_copy(ostage.at[p, 0], mixed.at[rows_of(p), own_columns], out_r.at[p])

    def finish(p):
        rows = rows_of(p)
        for first, last, done in REST:
            count = last - first
            total = acc[first:last, rows].reshape(count * PIECE, 256)
            q = qk[first:last, rows, :128].reshape(count * PIECE, 128)
            for at in range(done, 16, 4):
                total += weigh(q, at, min(at + 4, 16))
            ostage[p, first:last] = (total[:, :128] / total[:, 128:]).astype(BF16).reshape(count, PIECE, 128)

        @pl.when(stays)
        def _():
            keep_copy(p).start()

        @pl.when(jnp.logical_not(stays))
        def _():
            out_copy(p, 0).start()

        @pl.when(c == 0)
        def _():
            for place in range(1, 16):
                out_copy(p, place).start()

        @pl.when(c == 1)
        def _():
            for place in range(15, 0, -1):
                out_copy(p, place).start()

    def hand(src, dst, send, recv, p, to):
        return remote(src.at[rows_of(p)], dst.at[rows_of(p)], send.at[p], recv.at[p], to)

    above, below, _ = planes
    term_copy = lambda p: hand(pout, tin, t_s, t_r, p, sibling)
    sum_up = lambda p: hand(sout, in0, s0_s, s0_r, p, above)
    sum_wrap = lambda p: hand(sout, in0, s1_s, s0_r, p, below)
    sum_next = lambda p: hand(sout, in1, s1_s, s1_r, p, above)
    pass_down = lambda p: hand(in0, in0, s0_s, s0_r, p, below)
    back_in0 = lambda p: hand(in0, pin, e_s, e_r, p, sibling)
    back_pout = lambda p: hand(pout, pin, e_s, e_r, p, sibling)

    def load(ref, p):
        return ref[rows_of(p)].astype(F32)

    def begin(p):
        rows = rows_of(p)
        pltpu.make_async_copy(mixed.at[rows], mixed.at[rows], out_r.at[p]).wait()
        here = load(mixed, p)
        term = gd[...] * here
        vel[rows] = gate_row[...] * here
        pltpu.make_async_copy(vel.at[rows], vel_ref.at[rows], put_sem.at[0]).start()

        @pl.when(c == 0)
        def _():
            @pl.when(y == 0)
            def _():
                pout[rows] = (x_ref[rows] + term).astype(BF16)

            @pl.when(y > 0)
            def _():
                pout[rows] = term.astype(BF16)

            term_copy(p).start()

        @pl.when(c == 1)
        def _():
            term_copy(p).wait_recv()

            @pl.when(y < 2)
            def _():
                sout[rows] = (load(tin, p) + term).astype(BF16)

            @pl.when(y == 0)
            def _():
                sum_up(p).start()
                sum_wrap(p).start()

            @pl.when(y == 1)
            def _():
                sum_next(p).start()

            @pl.when(y == 2)
            def _():
                sout[rows] = (load(tin, p) + term).astype(BF16)

    def middle(p):
        rows = rows_of(p)

        @pl.when(jnp.logical_and(c == 1, y == 2))
        def _():
            sum_next(p).wait_recv()
            sout[rows] = (load(in1, p) + load(sout, p)).astype(BF16)
            sum_next(p).start()

        @pl.when(jnp.logical_and(c == 1, y == 3))
        def _():
            sum_up(p).wait_recv()
            pass_down(p).start()

    def end(p):
        rows = rows_of(p)

        term = gd[...] * load(mixed, p)

        @pl.when(step == 0)
        def _():
            new[rows] = x_ref[rows] + term

        @pl.when(jnp.logical_and(c == 0, y > 0))
        def _():
            back_in0(p).wait_recv()
            new[rows] = load(pin, p) + term

        @pl.when(jnp.logical_and(c == 1, y == 0))
        def _():
            new[rows] = load(tin, p) + term

        @pl.when(jnp.logical_and(c == 1, y == 1))
        def _():
            sum_up(p).wait_recv()
            back_in0(p).start()
            new[rows] = load(in0, p) + load(tin, p) + term

        @pl.when(jnp.logical_and(c == 1, y > 1))
        def _():
            @pl.when(y == 2)
            def _():
                pass_down(p).wait_recv()

            @pl.when(y == 3)
            def _():
                sum_next(p).wait_recv()

            total = load(in0, p) + load(in1, p)
            pout[rows] = total.astype(BF16)
            back_pout(p).start()
            new[rows] = total + load(tin, p) + term

        pltpu.make_async_copy(new.at[rows], new_ref.at[rows], put_sem.at[1]).start()

    def body(p, carry):
        @pl.when(p < PIECES)
        def _():
            finish(p)

        for lag, part in LAGS:
            @pl.when(jnp.logical_and(p >= lag, p < PIECES + lag))
            def _(lag=lag, part=part):
                stages[part](p - lag)
        return carry

    stages = {"begin": begin, "middle": middle, "end": end}
    lax.fori_loop(0, PIECES + LAGS[-1][0], body, 0)

    for copy in hops:
        copy.wait_send()
    for slot in shares:
        shares[slot].wait_send()

    @pl.when(stays)
    def _():
        for copy in home_out:
            copy.wait_send()
        pltpu.make_async_copy(ostage.at[:, 1:], ostage.at[:, 1:], out_s).wait()

    @pl.when(jnp.logical_not(stays))
    def _():
        pltpu.make_async_copy(ostage, ostage, out_s).wait()

    @pl.when(c == 1)
    def _():
        w_across.wait_send()
        for copy in w_planes:
            copy.wait_send()

    def drain(p, carry):
        @pl.when(c == 0)
        def _():
            term_copy(p).wait_send()

        @pl.when(c == 1)
        def _():
            @pl.when(y == 0)
            def _():
                sum_up(p).wait_send()
                sum_wrap(p).wait_send()

            @pl.when(jnp.logical_or(y == 1, y == 2))
            def _():
                sum_next(p).wait_send()

            @pl.when(y == 3)
            def _():
                pass_down(p).wait_send()

            @pl.when(y > 0)
            def _():
                back_in0(p).wait_send()
        return carry

    lax.fori_loop(0, PIECES, drain, 0)
    pltpu.make_async_copy(vel, vel_ref, put_sem.at[0]).wait()
    pltpu.make_async_copy(new, new_ref, put_sem.at[1]).wait()


def sweep(ids, sched, window, x, w, ae, md, mu):
    sm = pl.BlockSpec(memory_space=pltpu.SMEM)
    anywhere = pl.BlockSpec(memory_space=pl.ANY)
    dma = pltpu.SemaphoreType.DMA
    return pl.pallas_call(
        sweep_kernel,
        out_shape=(
            jax.ShapeDtypeStruct((256, 2048), F32), jax.ShapeDtypeStruct((256, 2048), F32),
        ),
        in_specs=[sm, sm, sm, anywhere, anywhere, anywhere, anywhere, anywhere],
        out_specs=(anywhere, anywhere),
        scratch_shapes=[
            pltpu.VMEM((256, 2048), BF16),
            pltpu.VMEM((256, 2048), BF16),
            pltpu.VMEM((256, 2048), F32),
            pltpu.VMEM((256, 2048), F32),
            pltpu.VMEM((256, 2048), F32),
            pltpu.VMEM((1, 2048), F32),
            pltpu.VMEM((16, 256, 2048), BF16),
            pltpu.VMEM((2048, 384), BF16),
            pltpu.VMEM((2048, 384), BF16),
            pltpu.VMEM((1, 384), F32),
            pltpu.VMEM((512, 2048), BF16),
            pltpu.VMEM((2048, 256), BF16),
            pltpu.VMEM((256, 6144), BF16),
            pltpu.VMEM((16, 256, 256), BF16),
            pltpu.VMEM((16, 256, 256), BF16),
            pltpu.VMEM((16, 256, 256), F32),
            pltpu.VMEM((PIECES, 16, PIECE, 128), BF16),
            pltpu.VMEM((256, 2048), BF16),
            pltpu.VMEM((1, 2048), F32),
            pltpu.VMEM((256, 2048), BF16),
            pltpu.VMEM((256, 2048), BF16),
            pltpu.VMEM((256, 2048), BF16),
            pltpu.VMEM((256, 2048), BF16),
            dma((5,)), dma((2,)), dma((2,)), dma((2,)), dma, dma((16,)), dma((16,)), dma((4,)), dma((4,)),
            dma((17,)), dma((17,)), dma, dma((PIECES,)),
            *[dma((PIECES,)) for _ in range(8)], dma((2,)),
        ],
        compiler_params=pltpu.CompilerParams(
            collective_id=1, has_side_effects=True, vmem_limit_bytes=60 * 1024 * 1024
        ),
    )(ids, sched, window, x, w, ae, md, mu)


def on_device(
    iterate,
    query_key_value_weight,
    modulation_down_weight,
    modulation_up_weight,
    action_embedding_matrix,
    action_token_index,
    sched,
    window,
):
    new_states, velocity = sweep(
        action_token_index,
        sched,
        window,
        iterate[0],
        query_key_value_weight[:, 0],
        action_embedding_matrix,
        modulation_down_weight,
        modulation_up_weight,
    )
    return (new_states[None], velocity[None])


def solution(mesh):
    placed = (P("step", "seq", None), P(None, "seq", None), P(), P(), P(), P(), P(), P())
    return jax.shard_map(
        on_device,
        mesh=mesh,
        in_specs=placed,
        out_specs=(P("step", "seq", None), P("step", "seq", None)),
        check_vma=False,
    )
```

```python
import math

import jax
import jax.numpy as jnp
from jax import lax
from jax.experimental import pallas as pl
from jax.experimental.pallas import tpu as pltpu
from jax.sharding import PartitionSpec as P

MESH = pl.DeviceIdType.MESH
F32, BF16 = jnp.float32, jnp.bfloat16
PIECES = 8
REST = ((0, 16, 8),)
LAGS = ((3, "begin"), (5, "middle"), (7, "end"))
PIECE = 256 // PIECES
GROUPS = ((0, 1, 12, 4, 2), (3, 5, 13), (6, 8, 9), (14, 15, 7), (10, 11))
ORDER = sum(GROUPS, ())
FACTOR = 2.5 / math.sqrt(128) * math.log2(math.e)


def remote(src, dst, send, recv, device):
    return pltpu.make_async_remote_copy(
        src_ref=src, dst_ref=dst, send_sem=send, recv_sem=recv, device_id=device, device_id_type=MESH
    )


def inverse_rms(value):
    return lax.rsqrt(jnp.mean(value * value, axis=-1, keepdims=True) + 1e-6)


def sweep_kernel(
    ids, sched, window, x_hbm, w_ref, ae_ref, md_ref, mu_ref,
    new_ref, vel_ref,
    mixed, pin, new, vel, x_ref, gate_row,
    xbuf, wraw, wmod, bias, ae, md, mu, qk, v1, acc, ostage, pout, gd, sout, tin, in0, in1,
    load_sem, home_s, home_r, guest_s, guest_r, share_s, share_r, wx_s, wx_r,
    hop_s, hop_r, out_s, out_r, t_s, t_r, s0_s, s0_r, s1_s, s1_r, e_s, e_r, put_sem,
):
    step, seq = lax.axis_index("step"), lax.axis_index("seq")
    y, c = step // 2, lax.rem(step, 2)
    z, x = seq // 4, lax.rem(seq, 4)
    m = x // 2
    stays = c == m
    head = jnp.where(c == 0, seq, z * 4 + 3 - x)

    def device(core, dz, column):
        return (y * 2 + core, lax.rem(z + dz + 4, 4) * 4 + column)

    x_load = pltpu.make_async_copy(x_hbm, x_ref, load_sem.at[4])
    x_load.start()
    mate = device(c, 0, x + 1 - 2 * lax.rem(x, 2))
    up, down = device(c, 1, x), device(c, -1, x)
    sibling = device(1 - c, 0, x)
    across = [device(core, 0, 3 - x) for core in range(2)]
    planes = [(lax.rem(y + dy, 4) * 2 + c, seq) for dy in (1, 3, 2)]

    barrier = pltpu.get_barrier_semaphore()
    for other in (mate, up, down, sibling, *across, *planes):
        pl.semaphore_signal(barrier, inc=1, device_id=other, device_id_type=MESH)
    for other_z in range(4):
        for column in range(2):
            for core in range(2):
                source = (y * 2 + core, other_z * 4 + 2 * c + column)
                itself = jnp.logical_and(core == c, other_z * 4 + 2 * c + column == seq)

                @pl.when(jnp.logical_not(itself))
                def _():
                    pl.semaphore_signal(barrier, inc=1, device_id=source, device_id_type=MESH)

    loads = [
        pltpu.make_async_copy(ae_ref, ae, load_sem.at[0]),
        pltpu.make_async_copy(md_ref, md, load_sem.at[1]),
        pltpu.make_async_copy(mu_ref, mu, load_sem.at[2]),
    ]
    for load in loads:
        load.start()
    own_w = pltpu.make_async_copy(w_ref, wraw, load_sem.at[3])

    @pl.when(c == 0)
    def _():
        own_w.start()

    mine = pl.ds(pl.multiple_of(c * 128, 128), 128)
    theirs = pl.ds(pl.multiple_of((1 - c) * 128, 128), 128)

    home_out = [
        remote(xbuf.at[0, theirs], xbuf.at[0, theirs], home_s.at[0], home_r.at[0], sibling),
        remote(xbuf.at[0, mine], xbuf.at[0, mine], home_s.at[1], home_r.at[1], sibling),
    ]
    guest_out = [
        remote(pout.at[pl.ds(core * 128, 128)], xbuf.at[1, pl.ds(core * 128, 128)], guest_s.at[core], guest_r, across[core])
        for core in range(2)
    ]

    pl.semaphore_wait(barrier, 9 + 16 - stays.astype(jnp.int32))

    quarter = pl.ds(pl.multiple_of(y * 512, 512), 512)
    w_across = remote(w_ref.at[quarter], wraw.at[quarter], wx_s.at[0], wx_r.at[0], across[1])
    w_planes = [
        remote(wraw.at[quarter], wraw.at[quarter], wx_s.at[i + 1], wx_r.at[i + 1], planes[i]) for i in range(3)
    ]

    @pl.when(c == 1)
    def _():
        w_across.start()

    x_load.wait()

    def unit(rows):
        value = x_ref[rows]
        return (value * inverse_rms(value)).astype(BF16)


    @pl.when(stays)
    def _():
        xbuf[0, theirs] = unit(theirs)
        home_out[0].start()
        xbuf[0, mine] = unit(mine)

    @pl.when(jnp.logical_not(stays))
    def _():
        for core in range(2):
            pout[core * 128:(core + 1) * 128] = unit(pl.ds(core * 128, 128))
            guest_out[core].start()
        home_out[0].wait_recv()

    hops = []

    def hop(index, slot, to, to_slot, first=0, count=128):
        rows = pl.ds(pl.multiple_of(c * 128 + first, 32), count)
        copy = remote(xbuf.at[slot, rows], xbuf.at[to_slot, rows], hop_s.at[index], hop_r.at[index], to)
        hops.append(copy)
        return copy

    shares = {}

    def share(slot):
        shares[slot] = remote(xbuf.at[slot, mine], xbuf.at[slot, mine], share_s.at[slot], share_r.at[slot], sibling)
        shares[slot].start()

    h01 = hop(0, 0, mate, 2)
    h30 = hop(1, 0, up, 12)
    h10 = hop(2, 0, down, 4)
    for copy in (h01, h30, h10):
        copy.start()

    @pl.when(stays)
    def _():
        home_out[1].start()

    stamps = [sched[window[2 * y + i]].astype(F32) for i in range(3)]
    row8 = lax.broadcasted_iota(jnp.int32, (8, 1024), 0)
    lane = lax.broadcasted_iota(jnp.int32, (8, 1024), 1).astype(F32)
    angles = jnp.where(row8 == 0, stamps[0], stamps[1]) * jnp.exp(-math.log(10000.0) / 1024 * lane)
    temb = jnp.concatenate([jnp.cos(angles), jnp.sin(angles)], axis=1)
    vocab = lax.broadcasted_iota(jnp.int32, (16, 512), 1)
    counts = jnp.zeros((16, 512), F32)
    for i in range(12):
        counts += (vocab == ids[i]).astype(F32)
    for load in loads:
        load.wait()
    mean = jnp.dot(counts.astype(BF16), ae[...], preferred_element_type=F32)[:8] / 12.0
    cond = temb + mean
    cond = (cond / (1.0 + jnp.exp(-cond))).astype(BF16)
    low = jnp.dot(cond, md[...], preferred_element_type=F32).astype(BF16)
    factors = jnp.dot(low, mu[...], preferred_element_type=F32)
    scale_cols = lax.dot_general(
        mu[:, 2048:4096], low, (((0,), (1,)), ((), ())), preferred_element_type=F32
    )
    rows = lax.broadcasted_iota(jnp.int32, (8, 2048), 0)
    gate = jnp.sum(jnp.where(rows == c, factors[:, 4096:], 0.0), axis=0, keepdims=True)
    delta = jnp.where(c == 0, stamps[1] / 1000.0 - stamps[0] / 1000.0, stamps[2] / 1000.0 - stamps[1] / 1000.0)
    gate_row[...] = gate
    gd[...] = gate * delta
    columns = lax.broadcasted_iota(jnp.int32, (2048, 8), 1)
    scale = jnp.sum(jnp.where(columns == m, scale_cols, 0.0), axis=1, keepdims=True)
    shift = factors[:, :2048]
    shift_high = shift.astype(BF16)
    shift_low = (shift - shift_high.astype(F32)).astype(BF16)

    @pl.when(c == 1)
    def _():
        w_across.wait_recv()
        for copy in w_planes:
            copy.start()

    guest_out[0].wait_recv()
    g01, g30, g10 = hop(3, 1, mate, 3), hop(4, 1, up, 13), hop(5, 1, down, 5)
    for copy in (g01, g30, g10):
        copy.start()
    share(1)
    h30.wait_recv()
    h20, x31h = hop(6, 12, up, 8), hop(7, 12, mate, 14)
    h20.start()
    x31h.start()
    share(12)
    h10.wait_recv()
    x11h = hop(8, 4, mate, 6)
    x11h.start()
    share(4)
    h01.wait_recv()
    share(2)

    g01.wait_recv()
    g31, g11 = hop(9, 3, up, 15), hop(10, 3, down, 7)
    g31.start()
    g11.start()
    share(3)
    g10.wait_recv()
    g20 = hop(11, 5, down, 9)
    g20.start()
    share(5)
    g30.wait_recv()
    share(13)

    @pl.when(c == 0)
    def _():
        own_w.wait()

    @pl.when(c == 1)
    def _():
        for copy in w_planes:
            copy.wait_recv()

    for i in range(4):
        part = pl.ds(i * 512, 512)
        wmod[part] = (wraw[part].astype(F32) * (1.0 + scale[i * 512:(i + 1) * 512])).astype(BF16)
    shifted = jnp.dot(shift_high, wraw[...], preferred_element_type=F32)
    shifted += jnp.dot(shift_low, wraw[...], preferred_element_type=F32)
    rows = lax.broadcasted_iota(jnp.int32, (8, 384), 0)
    bias[...] = jnp.sum(jnp.where(rows == m, shifted, 0.0), axis=0, keepdims=True)
    v1[:, :, 128:] = jnp.ones((16, 256, 128), BF16)

    def block_of(slot):
        zr, kind = slot // 4, slot % 4
        other = x + 1 - 2 * lax.rem(x, 2)
        return lax.rem(z + zr, 4) * 4 + (x, 3 - x, other, 3 - other)[kind]

    def project(slot):
        place = ORDER.index(slot)
        p = jnp.dot(xbuf[slot], wmod[...], preferred_element_type=F32) + bias[...]
        q, k = p[:, :128], p[:, 128:256]
        qk[place, :, :128] = (q * (inverse_rms(q) * FACTOR)).astype(BF16)
        qk[place, :, 128:] = (k * inverse_rms(k)).astype(BF16)
        v1[place, :, :128] = p[:, 256:].astype(BF16)

    def weigh(q, first, last):
        keys = qk[first:last, :, 128:].reshape((last - first) * 256, 128)
        values = v1[first:last].reshape((last - first) * 256, 256)
        s = lax.dot_general(q, keys, (((1,), (1,)), ((), ())), preferred_element_type=F32)
        return jnp.dot(jnp.exp2(s).astype(BF16), values, preferred_element_type=F32)

    def fresh(first, last):
        count = last - first
        q = qk[first:last, :, :128].reshape(count * 256, 128)
        for at in range(0, min(last, 8), 4):
            part = weigh(q, at, min(at + 4, last)).reshape(count, 256, 256)
            if at == 0:
                acc[first:last] = part
            else:
                acc[first:last] += part

    def extend(first, last):
        for half in range(2):
            rows = pl.ds(half * 128, 128)
            q = qk[:first, rows, :128].reshape(first * 128, 128)
            acc[:first, rows] += weigh(q, first, last).reshape(first, 128, 256)

    def absorb(group):
        first = ORDER.index(GROUPS[group][0])
        last = first + len(GROUPS[group])
        for slot in GROUPS[group]:
            if slot:
                shares[slot].wait_recv()
            else:
                @pl.when(jnp.logical_not(stays))
                def _():
                    home_out[1].wait_recv()
            project(slot)
        if 0 < group < 2:
            extend(first, last)
        fresh(first, last)

    absorb(0)
    absorb(1)
    x11h.wait_recv()
    part11 = hop(12, 6, down, 10, 32, 32)
    part11.start()
    share(6)
    h20.wait_recv()
    part20 = hop(13, 8, mate, 10, 64, 64)
    part20.start()
    share(8)
    g20.wait_recv()
    share(9)
    x31h.wait_recv()
    part31 = hop(14, 14, up, 10, 0, 32)
    part31.start()
    share(14)
    g31.wait_recv()
    part31g = hop(15, 15, up, 11, 0, 64)
    part31g.start()
    share(15)
    g11.wait_recv()
    part11g = hop(16, 7, down, 11, 64, 64)
    part11g.start()
    share(7)
    absorb(2)
    absorb(3)
    part31.wait_recv()
    part11.wait_recv()
    part20.wait_recv()
    share(10)
    part31g.wait_recv()
    part11g.wait_recv()
    share(11)
    absorb(4)

    @pl.when(jnp.logical_not(stays))
    def _():
        for copy in guest_out:
            copy.wait_send()


    own_columns = pl.ds(pl.multiple_of(head * 128, 128), 128)
    dests = [block_of(slot) for slot in ORDER]

    def rows_of(p):
        return pl.ds(pl.multiple_of(p * PIECE, PIECE), PIECE)

    def out_copy(p, place):
        return remote(
            ostage.at[p, place], mixed.at[rows_of(p), own_columns], out_s, out_r.at[p], (y * 2 + m, dests[place])
        )

    def keep_copy(p):
        return pltpu.make_async_copy(ostage.at[p, 0], mixed.at[rows_of(p), own_columns], out_r.at[p])

    def finish(p):
        rows = rows_of(p)
        for first, last, done in REST:
            count = last - first
            total = acc[first:last, rows].reshape(count * PIECE, 256)
            q = qk[first:last, rows, :128].reshape(count * PIECE, 128)
            for at in range(done, 16, 4):
                total += weigh(q, at, min(at + 4, 16))
            ostage[p, first:last] = (total[:, :128] / total[:, 128:]).astype(BF16).reshape(count, PIECE, 128)

        @pl.when(stays)
        def _():
            keep_copy(p).start()

        @pl.when(jnp.logical_not(stays))
        def _():
            out_copy(p, 0).start()

        @pl.when(c == 0)
        def _():
            for place in range(1, 16):
                out_copy(p, place).start()

        @pl.when(c == 1)
        def _():
            for place in range(15, 0, -1):
                out_copy(p, place).start()

    def hand(src, dst, send, recv, p, to):
        return remote(src.at[rows_of(p)], dst.at[rows_of(p)], send.at[p], recv.at[p], to)

    above, below, _ = planes
    term_copy = lambda p: hand(pout, tin, t_s, t_r, p, sibling)
    sum_up = lambda p: hand(sout, in0, s0_s, s0_r, p, above)
    sum_wrap = lambda p: hand(sout, in0, s1_s, s0_r, p, below)
    sum_next = lambda p: hand(sout, in1, s1_s, s1_r, p, above)
    pass_down = lambda p: hand(in0, in0, s0_s, s0_r, p, below)
    back_in0 = lambda p: hand(in0, pin, e_s, e_r, p, sibling)
    back_pout = lambda p: hand(pout, pin, e_s, e_r, p, sibling)

    def load(ref, p):
        return ref[rows_of(p)].astype(F32)

    def begin(p):
        rows = rows_of(p)
        pltpu.make_async_copy(mixed.at[rows], mixed.at[rows], out_r.at[p]).wait()
        here = load(mixed, p)
        term = gd[...] * here
        vel[rows] = gate_row[...] * here
        pltpu.make_async_copy(vel.at[rows], vel_ref.at[rows], put_sem.at[0]).start()

        @pl.when(c == 0)
        def _():
            @pl.when(y == 0)
            def _():
                pout[rows] = (x_ref[rows] + term).astype(BF16)

            @pl.when(y > 0)
            def _():
                pout[rows] = term.astype(BF16)

            term_copy(p).start()

        @pl.when(c == 1)
        def _():
            term_copy(p).wait_recv()

            @pl.when(y < 2)
            def _():
                sout[rows] = (load(tin, p) + term).astype(BF16)

            @pl.when(y == 0)
            def _():
                sum_up(p).start()
                sum_wrap(p).start()

            @pl.when(y == 1)
            def _():
                sum_next(p).start()

            @pl.when(y == 2)
            def _():
                sout[rows] = (load(tin, p) + term).astype(BF16)

    def middle(p):
        rows = rows_of(p)

        @pl.when(jnp.logical_and(c == 1, y == 2))
        def _():
            sum_next(p).wait_recv()
            sout[rows] = (load(in1, p) + load(sout, p)).astype(BF16)
            sum_next(p).start()

        @pl.when(jnp.logical_and(c == 1, y == 3))
        def _():
            sum_up(p).wait_recv()
            pass_down(p).start()

    def end(p):
        rows = rows_of(p)

        term = gd[...] * load(mixed, p)

        @pl.when(step == 0)
        def _():
            new[rows] = x_ref[rows] + term

        @pl.when(jnp.logical_and(c == 0, y > 0))
        def _():
            back_in0(p).wait_recv()
            new[rows] = load(pin, p) + term

        @pl.when(jnp.logical_and(c == 1, y == 0))
        def _():
            new[rows] = load(tin, p) + term

        @pl.when(jnp.logical_and(c == 1, y == 1))
        def _():
            sum_up(p).wait_recv()
            back_in0(p).start()
            new[rows] = load(in0, p) + load(tin, p) + term

        @pl.when(jnp.logical_and(c == 1, y > 1))
        def _():
            @pl.when(y == 2)
            def _():
                pass_down(p).wait_recv()

            @pl.when(y == 3)
            def _():
                sum_next(p).wait_recv()

            total = load(in0, p) + load(in1, p)
            pout[rows] = total.astype(BF16)
            back_pout(p).start()
            new[rows] = total + load(tin, p) + term

        pltpu.make_async_copy(new.at[rows], new_ref.at[rows], put_sem.at[1]).start()

    def body(p, carry):
        @pl.when(p < PIECES)
        def _():
            finish(p)

        for lag, part in LAGS:
            @pl.when(jnp.logical_and(p >= lag, p < PIECES + lag))
            def _(lag=lag, part=part):
                stages[part](p - lag)
        return carry

    stages = {"begin": begin, "middle": middle, "end": end}
    lax.fori_loop(0, PIECES + LAGS[-1][0], body, 0)

    for copy in hops:
        copy.wait_send()
    for slot in shares:
        shares[slot].wait_send()

    @pl.when(stays)
    def _():
        for copy in home_out:
            copy.wait_send()
        pltpu.make_async_copy(ostage.at[:, 1:], ostage.at[:, 1:], out_s).wait()

    @pl.when(jnp.logical_not(stays))
    def _():
        pltpu.make_async_copy(ostage, ostage, out_s).wait()

    @pl.when(c == 1)
    def _():
        w_across.wait_send()
        for copy in w_planes:
            copy.wait_send()

    def drain(p, carry):
        @pl.when(c == 0)
        def _():
            term_copy(p).wait_send()

        @pl.when(c == 1)
        def _():
            @pl.when(y == 0)
            def _():
                sum_up(p).wait_send()
                sum_wrap(p).wait_send()

            @pl.when(jnp.logical_or(y == 1, y == 2))
            def _():
                sum_next(p).wait_send()

            @pl.when(y == 3)
            def _():
                pass_down(p).wait_send()

            @pl.when(y > 0)
            def _():
                back_in0(p).wait_send()
        return carry

    lax.fori_loop(0, PIECES, drain, 0)
    pltpu.make_async_copy(vel, vel_ref, put_sem.at[0]).wait()
    pltpu.make_async_copy(new, new_ref, put_sem.at[1]).wait()


def sweep(ids, sched, window, x, w, ae, md, mu):
    sm = pl.BlockSpec(memory_space=pltpu.SMEM)
    anywhere = pl.BlockSpec(memory_space=pl.ANY)
    dma = pltpu.SemaphoreType.DMA
    return pl.pallas_call(
        sweep_kernel,
        out_shape=(
            jax.ShapeDtypeStruct((256, 2048), F32), jax.ShapeDtypeStruct((256, 2048), F32),
        ),
        in_specs=[sm, sm, sm, anywhere, anywhere, anywhere, anywhere, anywhere],
        out_specs=(anywhere, anywhere),
        scratch_shapes=[
            pltpu.VMEM((256, 2048), BF16),
            pltpu.VMEM((256, 2048), BF16),
            pltpu.VMEM((256, 2048), F32),
            pltpu.VMEM((256, 2048), F32),
            pltpu.VMEM((256, 2048), F32),
            pltpu.VMEM((1, 2048), F32),
            pltpu.VMEM((16, 256, 2048), BF16),
            pltpu.VMEM((2048, 384), BF16),
            pltpu.VMEM((2048, 384), BF16),
            pltpu.VMEM((1, 384), F32),
            pltpu.VMEM((512, 2048), BF16),
            pltpu.VMEM((2048, 256), BF16),
            pltpu.VMEM((256, 6144), BF16),
            pltpu.VMEM((16, 256, 256), BF16),
            pltpu.VMEM((16, 256, 256), BF16),
            pltpu.VMEM((16, 256, 256), F32),
            pltpu.VMEM((PIECES, 16, PIECE, 128), BF16),
            pltpu.VMEM((256, 2048), BF16),
            pltpu.VMEM((1, 2048), F32),
            pltpu.VMEM((256, 2048), BF16),
            pltpu.VMEM((256, 2048), BF16),
            pltpu.VMEM((256, 2048), BF16),
            pltpu.VMEM((256, 2048), BF16),
            dma((5,)), dma((2,)), dma((2,)), dma((2,)), dma, dma((16,)), dma((16,)), dma((4,)), dma((4,)),
            dma((17,)), dma((17,)), dma, dma((PIECES,)),
            *[dma((PIECES,)) for _ in range(8)], dma((2,)),
        ],
        compiler_params=pltpu.CompilerParams(
            collective_id=1, has_side_effects=True, vmem_limit_bytes=60 * 1024 * 1024
        ),
    )(ids, sched, window, x, w, ae, md, mu)


def on_device(
    iterate,
    query_key_value_weight,
    modulation_down_weight,
    modulation_up_weight,
    action_embedding_matrix,
    action_token_index,
    sched,
    window,
):
    new_states, velocity = sweep(
        action_token_index,
        sched,
        window,
        iterate[0],
        query_key_value_weight[:, 0],
        action_embedding_matrix,
        modulation_down_weight,
        modulation_up_weight,
    )
    return (new_states[None], velocity[None])


def solution(mesh):
    placed = (P("step", "seq", None), P(None, "seq", None), P(), P(), P(), P(), P(), P())
    return jax.shard_map(
        on_device,
        mesh=mesh,
        in_specs=placed,
        out_specs=(P("step", "seq", None), P("step", "seq", None)),
        check_vma=False,
    )
```
